512 devices in a mesh: batch: 32 (over z, core), feat: 16 (over y, x).
Axes of the slice: x: 4, y: 4, z: 16, core: 2. Of those that a mesh axis runs over, the one named last changes fastest.
Arguments:
- view_one: bfloat16 [512, 16384], P('batch', 'feat'), may hold values from -700 to 700, as said below
- view_two: bfloat16 [512, 16384], P('batch', 'feat'), may hold values from -700 to 700
Outputs:
- row_loss: float32 [16384], P('feat')
- grad_one: float32 [512, 16384], P('batch', 'feat')
- grad_two: float32 [512, 16384], P('batch', 'feat')
The draws below stay inside these ranges and needn't reach their ends.
Inputs may be any that keep to these rules, and one draw needn't show every extreme that they name: Both views of a row come from one image: every column of view_two is correlated with the same column of view_one.
All inputs are finite; a program needn't handle non-finite values.
Results may differ from the reference program's by a relative error of at most 0.01.
Values may be sent and summed in bfloat16 or wider, within the bound.
No kernel may reach another device: no remote copies, remote signals or barrier semaphores. Data moves between devices by JAX's collectives and lax.ppermute only.
A program may use at most 64 MiB of HBM per device.

```python
import math
import jax
import jax.numpy as jnp
from jax import lax

FEATURES = 16384
BATCH = 512


def shared_views(key, rise_top):
    keys = jax.random.split(key, 4)
    normal_base = jnp.clip(jax.random.normal(keys[0], (BATCH, FEATURES), jnp.float32), -4.0, 4.0)
    base = normal_base
    normal_other = jnp.clip(jax.random.normal(keys[1], (BATCH, FEATURES), jnp.float32), -4.0, 4.0)
    other = normal_other
    positions = jnp.arange(BATCH, dtype=jnp.float32) / max(BATCH - 1, 1)
    row_rise = 1.0 + (rise_top - 1.0) * positions
    row_spread = jnp.exp(jax.random.uniform(keys[2], (BATCH,), jnp.float32, 0.0, math.log(10.0)))
    row_scaling = (row_rise * row_spread)[:, None]
    linked = jax.random.uniform(keys[3], (FEATURES,), jnp.float32, 0.3, 0.95)
    return (base, other, linked, row_scaling)


def column_terms(key):
    keys = jax.random.split(key, 2)
    col_scaling = jnp.exp(jax.random.uniform(keys[0], (FEATURES,), jnp.float32, math.log(0.3), math.log(3.0)))
    col_center = jax.random.uniform(keys[1], (FEATURES,), jnp.float32, -2.0, 2.0)
    return (col_scaling, col_center)


def draw_view_one(key, part):
    rise_top = 3.0
    base, other, linked, row_scaling = shared_views(key, rise_top)
    key = jax.random.fold_in(key, 11)
    col_scaling, col_center = column_terms(key)
    return (col_scaling * (row_scaling * base + col_center)).astype(jnp.bfloat16)


def draw_view_two(key, part):
    rise_top = 3.0
    base, other, linked, row_scaling = shared_views(key, rise_top)
    key = jax.random.fold_in(key, 23)
    col_scaling, col_center = column_terms(key)
    joined = linked * base + jnp.sqrt(1.0 - linked * linked) * other
    return (col_scaling * (row_scaling * joined + col_center)).astype(jnp.bfloat16)


def setup_inputs(seed: int = 0) -> dict:
    streams_of = jax.random.split(jax.random.key(seed), 3)
    view_one = draw_view_one(jax.random.fold_in(streams_of[2], 71), 0)
    view_two = draw_view_two(jax.random.fold_in(streams_of[2], 71), 0)
    return dict(view_one=view_one, view_two=view_two)


EPSILON = 1e-05
LAMBDA = 0.0051

def normalize(source):
    values = source.astype(jnp.float32)
    center = lax.optimization_barrier(jnp.sum(values, axis=0)) / BATCH
    shifted = values - center
    spread = lax.optimization_barrier(jnp.sum(shifted * shifted, axis=0)) / BATCH
    scaling = lax.rsqrt(spread + EPSILON)
    return ((shifted * scaling).astype(jnp.bfloat16), scaling)

def batch_back(upstream, normed, scaling):
    first_mean = lax.optimization_barrier(jnp.sum(upstream, axis=0)) / BATCH
    second_mean = lax.optimization_barrier(jnp.sum(upstream * normed, axis=0)) / BATCH
    return scaling * (upstream - first_mean - normed * second_mean)

def reference(view_one, view_two):
    normed_one, scaling_one = normalize(view_one)
    normed_two, scaling_two = normalize(view_two)
    float_one = normed_one.astype(jnp.float32)
    float_two = normed_two.astype(jnp.float32)
    block_size = 1024 if FEATURES % 1024 == 0 else FEATURES
    block_count = FEATURES // block_size
    columns = jnp.arange(FEATURES, dtype=jnp.int32)

    def advance(running, block_index):
        first_col = (block_index * block_size).astype(jnp.int32)
        feature_rows = lax.dynamic_slice_in_dim(normed_one, first_col, block_size, 1)
        correlation = jnp.dot(feature_rows.T, normed_two, preferred_element_type=jnp.float32) / BATCH
        global_rows = first_col + jnp.arange(block_size, dtype=jnp.int32)
        diag_mask = global_rows[:, None] == columns[None, :]
        on_diag = lax.optimization_barrier(jnp.sum(jnp.where(diag_mask, correlation, 0.0), axis=1))
        off_squares = lax.optimization_barrier(jnp.sum(jnp.where(diag_mask, 0.0, correlation * correlation), axis=1))
        row_terms = (1.0 - on_diag) * (1.0 - on_diag) + LAMBDA * off_squares
        slopes = jnp.where(diag_mask, -2.0 * (1.0 - correlation), 2.0 * LAMBDA * correlation)
        first_block = jnp.dot(float_two, slopes.T, precision=lax.Precision.HIGHEST)
        running = running + jnp.dot(feature_rows.astype(jnp.float32), slopes, precision=lax.Precision.HIGHEST)
        return (running, (row_terms, first_block))
    second_up, (row_terms, first_blocks) = lax.scan(advance, jnp.zeros((BATCH, FEATURES), jnp.float32), jnp.arange(block_count, dtype=jnp.int32))
    row_loss = row_terms.reshape(FEATURES)
    first_up = jnp.transpose(first_blocks, (1, 0, 2)).reshape(BATCH, FEATURES)
    grad_one = batch_back(first_up, float_one, scaling_one)
    grad_two = batch_back(second_up, float_two, scaling_two)
    return (row_loss, grad_one, grad_two)
```

```python
import jax
import jax.numpy as jnp
from jax import lax
from jax.sharding import Mesh, PartitionSpec as P

EPSILON = 1e-05
LAMBDA = 0.0051
FEATURES = 16384
BATCH = 512

CUTS = (4, 4, 2, 4, 4)
NAMES = ("zh", "zl", "c", "y", "x")
CHIPS = ("zh", "zl")
FEAT = ("y", "x")
SLICES = 4


def swap(values, axes):
    return lax.all_to_all(values, axes, split_axis=0, concat_axis=0)


def local(view_one, view_two):
    rows, width = view_one.shape
    part = width // SLICES
    core = lax.axis_index("c")
    group = lax.axis_index("zh")

    both = jnp.stack([view_one, view_two]).reshape(2, rows, SLICES, part)
    both = jnp.transpose(both, (2, 0, 1, 3))
    sent = jnp.broadcast_to(both[None], (4,) + both.shape).reshape(16, 2, rows, part)
    chips = swap(sent, CHIPS)
    whole = lax.all_gather(chips, "c")
    views = jnp.transpose(whole, (2, 0, 1, 3, 4)).reshape(2, BATCH, part)

    values = views.astype(jnp.float32)
    center = jnp.sum(values, axis=1, keepdims=True) / BATCH
    shifted = values - center
    spread = jnp.sum(shifted * shifted, axis=1, keepdims=True) / BATCH
    scaling = lax.rsqrt(spread + EPSILON)
    normed = (shifted * scaling).astype(jnp.bfloat16)
    mine = lax.dynamic_index_in_dim(normed, core, 0, keepdims=False)
    other = lax.dynamic_index_in_dim(normed, 1 - core, 0, keepdims=False)
    scale_mine = lax.dynamic_index_in_dim(scaling, core, 0, keepdims=False)

    eye = jnp.eye(BATCH, dtype=jnp.float32)
    gram = lax.dot_general(
        other, other, (((1,), (1,)), ((), ())), preferred_element_type=jnp.float32
    )
    gram = (gram - part * eye).astype(jnp.bfloat16).reshape(16, BATCH // 16, BATCH)
    strip = jnp.sum(swap(gram, FEAT).astype(jnp.float32), axis=0).astype(jnp.bfloat16)
    strip = swap(jnp.broadcast_to(strip[None], (SLICES,) + strip.shape), "zl")
    strip = jnp.sum(strip.astype(jnp.float32), axis=0).astype(jnp.bfloat16)
    total = swap(jnp.broadcast_to(strip[None], (16,) + strip.shape), FEAT).reshape(BATCH, BATCH)

    float_mine = mine.astype(jnp.float32)
    float_other = other.astype(jnp.float32)
    on_diag = jnp.sum(float_mine * float_other, axis=0, keepdims=True) / BATCH
    slope = -2.0 * (1.0 - on_diag) - 2.0 * LAMBDA * on_diag
    product = jnp.dot(total, mine, preferred_element_type=jnp.float32) + FEATURES * float_mine
    squares = jnp.sum(product * float_mine, axis=0, keepdims=True) / (BATCH * BATCH)
    loss = (1.0 - on_diag) * (1.0 - on_diag) + LAMBDA * (squares - on_diag * on_diag)
    up = (2.0 * LAMBDA / BATCH) * product + slope * float_other
    first = jnp.sum(up, axis=0, keepdims=True) / BATCH
    second = jnp.sum(up * float_mine, axis=0, keepdims=True) / BATCH
    grad = scale_mine * (up - first - float_mine * second)

    grad = grad.reshape(2, 4, 4, rows, part)
    grad = lax.dynamic_index_in_dim(grad, group, 1, keepdims=False)
    grad = jnp.transpose(grad, (1, 0, 2, 3)).reshape(8, rows, part).astype(jnp.bfloat16)
    high = loss.astype(jnp.bfloat16)
    rest = loss - high.astype(jnp.float32)
    middle = rest.astype(jnp.bfloat16)
    low = (rest - middle.astype(jnp.float32)).astype(jnp.bfloat16)
    tail = jnp.concatenate([high, middle, low, jnp.zeros((13, part), jnp.bfloat16)], axis=0)
    tail = jnp.broadcast_to(tail[None], (8,) + tail.shape)
    out = swap(jnp.concatenate([grad, tail], axis=1), ("zl", "c")).astype(jnp.float32)
    out = out.reshape(SLICES, 2, rows + 16, part)
    row_loss = (out[:, 0, rows] + (out[:, 0, rows + 1] + out[:, 0, rows + 2])).reshape(width)
    grads = jnp.transpose(out[:, :, :rows], (1, 2, 0, 3)).reshape(2, rows, width)
    return (row_loss, grads[0], grads[1])


def solution(mesh):
    cut = Mesh(mesh.devices.reshape(CUTS), NAMES)
    spread = P(("zh", "zl", "c"), FEAT)
    return jax.shard_map(
        local, mesh=cut, in_specs=(spread, spread), out_specs=(P(FEAT), spread, spread), check_vma=False
    )
```

```python
import jax
import jax.numpy as jnp
from jax import lax
from jax.experimental import pallas as pl
from jax.experimental.pallas import tpu as pltpu
from jax.sharding import Mesh, PartitionSpec as P

EPSILON = 1e-05
LAMBDA = 0.0051
FEATURES = 16384
BATCH = 512

CUTS = (4, 4, 2, 4, 4)
NAMES = ("zh", "zl", "c", "y", "x")
CHIPS = ("zh", "zl")
FEAT = ("y", "x")
GROUPS = 4
SLICES = 4
OWNERS = 16
ROWS = 16
WIDTH = 1024
PART = WIDTH // SLICES
SIDE = 128
BLOCKS = BATCH // SIDE
PACKED = BLOCKS * (BLOCKS + 1) // 2 * SIDE
CHUNK = PACKED // OWNERS
NT = (((1,), (1,)), ((), ()))
TN = (((0,), (0,)), ((), ()))


def swap(values, axes):
    return lax.all_to_all(values, axes, split_axis=0, concat_axis=0)


def place(i, j):
    return (i * (i + 1) // 2 + j) * SIDE


def call(kernel, out_shape, flops, *operands, scratch=(), scalars=0):
    moved = sum(o.size * o.dtype.itemsize for o in operands)
    specs = [pl.BlockSpec(memory_space=pltpu.SMEM)] * scalars
    specs += [pl.BlockSpec(memory_space=pltpu.VMEM)] * (len(operands) - scalars)
    many = isinstance(out_shape, (list, tuple))
    whole = pl.BlockSpec(memory_space=pltpu.VMEM)
    return pl.pallas_call(
        kernel,
        out_shape=out_shape,
        in_specs=specs,
        out_specs=[whole] * len(out_shape) if many else whole,
        scratch_shapes=list(scratch),
        cost_estimate=pl.CostEstimate(flops=flops, bytes_accessed=moved, transcendentals=0),
        compiler_params=pltpu.CompilerParams(vmem_limit_bytes=16 * 1024 * 1024),
    )(*operands)


def spread_kernel(one_ref, two_ref, out_ref):
    for k in range(SLICES):
        columns = slice(k * PART, (k + 1) * PART)
        one, two = one_ref[:, columns], two_ref[:, columns]
        for h in range(GROUPS):
            out_ref[h * SLICES + k, 0] = one
            out_ref[h * SLICES + k, 1] = two


def gram_kernel(core_ref, whole_ref, normed_ref, scaling_ref, packed_ref):
    for v in range(2):
        values = whole_ref[:, v].astype(jnp.float32).reshape(BATCH, PART)
        center = jnp.sum(values, axis=0, keepdims=True) / BATCH
        shifted = values - center
        spread = jnp.sum(shifted * shifted, axis=0, keepdims=True) / BATCH
        scaling = lax.rsqrt(spread + EPSILON)
        scaling_ref[v] = scaling
        normed_ref[v] = (shifted * scaling).astype(jnp.bfloat16)
    other = 1 - core_ref[0]
    row = lax.broadcasted_iota(jnp.int32, (SIDE, SIDE), 0)
    column = lax.broadcasted_iota(jnp.int32, (SIDE, SIDE), 1)
    mean_diag = jnp.where(row == column, float(PART), 0.0)
    for i in range(BLOCKS):
        left = normed_ref[other, i * SIDE : (i + 1) * SIDE]
        for j in range(i + 1):
            right = normed_ref[other, j * SIDE : (j + 1) * SIDE]
            block = lax.dot_general(left, right, NT, preferred_element_type=jnp.float32)
            if i == j:
                block = block - mean_diag
            packed_ref[place(i, j) : place(i, j) + SIDE] = block.astype(jnp.bfloat16)


def sum_kernel(parts_ref, out_ref):
    total = parts_ref[0].astype(jnp.float32)
    for k in range(1, parts_ref.shape[0]):
        total = total + parts_ref[k].astype(jnp.float32)
    total = total.astype(jnp.bfloat16)
    for k in range(out_ref.shape[0]):
        out_ref[k] = total


def apply_kernel(place_ref, packed_ref, normed_ref, scaling_ref, out_ref, up_ref):
    core, group = place_ref[0], place_ref[1]
    mine = [normed_ref[core, i * SIDE : (i + 1) * SIDE] for i in range(BLOCKS)]
    zero = jnp.zeros((1, PART), jnp.float32)
    on_diag = zero
    for i in range(BLOCKS):
        other = normed_ref[1 - core, i * SIDE : (i + 1) * SIDE].astype(jnp.float32)
        on_diag = on_diag + jnp.sum(mine[i].astype(jnp.float32) * other, axis=0, keepdims=True)
    on_diag = on_diag / BATCH
    slope = -2.0 * (1.0 - on_diag) - 2.0 * LAMBDA * on_diag
    squares, first, second = zero, zero, zero
    for i in range(BLOCKS):
        held = mine[i].astype(jnp.float32)
        product = FEATURES * held
        for j in range(BLOCKS):
            if i >= j:
                block = packed_ref[place(i, j) : place(i, j) + SIDE]
                product = product + jnp.dot(block, mine[j], preferred_element_type=jnp.float32)
            else:
                block = packed_ref[place(j, i) : place(j, i) + SIDE]
                product = product + lax.dot_general(
                    block, mine[j], TN, preferred_element_type=jnp.float32
                )
        other = normed_ref[1 - core, i * SIDE : (i + 1) * SIDE].astype(jnp.float32)
        up = (2.0 * LAMBDA / BATCH) * product + slope * other
        up_ref[i * SIDE : (i + 1) * SIDE] = up
        squares = squares + jnp.sum(product * held, axis=0, keepdims=True)
        first = first + jnp.sum(up, axis=0, keepdims=True)
        second = second + jnp.sum(up * held, axis=0, keepdims=True)
    squares, first, second = squares / (BATCH * BATCH), first / BATCH, second / BATCH
    loss = (1.0 - on_diag) * (1.0 - on_diag) + LAMBDA * (squares - on_diag * on_diag)
    scaling = scaling_ref[core]
    for k in range(SLICES):
        for c in range(2):
            start = c * (BATCH // 2) + (group * SLICES + k) * ROWS
            rows = pl.ds(pl.multiple_of(start, ROWS), ROWS)
            held = normed_ref[core, rows].astype(jnp.float32)
            grad = scaling * (up_ref[rows] - first - held * second)
            out_ref[2 * k + c, :ROWS] = grad.astype(jnp.bfloat16)
    high = loss.astype(jnp.bfloat16)
    rest = loss - high.astype(jnp.float32)
    middle = rest.astype(jnp.bfloat16)
    low = (rest - middle.astype(jnp.float32)).astype(jnp.bfloat16)
    index = lax.broadcasted_iota(jnp.int32, (ROWS, PART), 0)
    terms = [jnp.broadcast_to(t.astype(jnp.float32), (ROWS, PART)) for t in (high, middle, low)]
    tail = jnp.where(index == 0, terms[0], jnp.where(index == 1, terms[1], terms[2]))
    tail = tail.astype(jnp.bfloat16)
    for k in range(2 * SLICES):
        out_ref[k, ROWS:] = tail


def unpack_kernel(parts_ref, loss_ref, one_ref, two_ref):
    for k in range(SLICES):
        columns = slice(k * PART, (k + 1) * PART)
        one_ref[:, columns] = parts_ref[2 * k, :ROWS].astype(jnp.float32)
        two_ref[:, columns] = parts_ref[2 * k + 1, :ROWS].astype(jnp.float32)
        tail = parts_ref[2 * k, ROWS:].astype(jnp.float32)
        loss_ref[:, columns] = tail[0:1] + (tail[1:2] + tail[2:3])


def local(view_one, view_two):
    bf16, f32 = jnp.bfloat16, jnp.float32
    shape = jax.ShapeDtypeStruct
    core = lax.axis_index("c").astype(jnp.int32)
    group = lax.axis_index("zh").astype(jnp.int32)
    where = jnp.stack([core, group])

    sent = call(spread_kernel, shape((OWNERS, 2, ROWS, PART), bf16), 0, view_one, view_two)
    whole = lax.all_gather(swap(sent, CHIPS), "c", axis=0, tiled=True)

    normed, scaling, packed = call(
        gram_kernel,
        [shape((2, BATCH, PART), bf16), shape((2, 1, PART), f32), shape((PACKED, SIDE), bf16)],
        2 * BATCH * BATCH * PART,
        where,
        whole,
        scalars=1,
    )
    strips = swap(packed.reshape(OWNERS, CHUNK, SIDE), FEAT)
    strips = swap(call(sum_kernel, shape((SLICES, CHUNK, SIDE), bf16), 0, strips), "zl")
    strips = swap(call(sum_kernel, shape((OWNERS, CHUNK, SIDE), bf16), 0, strips), FEAT)

    out = call(
        apply_kernel,
        shape((2 * SLICES, 2 * ROWS, PART), bf16),
        2 * BATCH * BATCH * PART,
        where,
        strips.reshape(PACKED, SIDE),
        normed,
        scaling,
        scratch=[pltpu.VMEM((BATCH, PART), f32)],
        scalars=1,
    )
    loss, one, two = call(
        unpack_kernel,
        [shape((1, WIDTH), f32), shape((ROWS, WIDTH), f32), shape((ROWS, WIDTH), f32)],
        0,
        swap(out, ("zl", "c")),
    )
    return (loss.reshape(WIDTH), one, two)


def solution(mesh):
    cut = Mesh(mesh.devices.reshape(CUTS), NAMES)
    spread = P(("zh", "zl", "c"), FEAT)
    return jax.shard_map(
        local, mesh=cut, in_specs=(spread, spread), out_specs=(P(FEAT), spread, spread), check_vma=False
    )
```

```python
import jax
import jax.numpy as jnp
from jax import lax
from jax.experimental import pallas as pl
from jax.experimental.pallas import tpu as pltpu
from jax.sharding import Mesh, PartitionSpec as P

EPSILON = 1e-05
LAMBDA = 0.0051
FEATURES = 16384
BATCH = 512

CUTS = (4, 4, 2, 4, 4)
NAMES = ("zh", "zl", "c", "y", "x")
IMAGES = ("zh", "zl", "c")
FEAT = ("y", "x")
GROUPS = 4
SLICES = 4
OWNERS = 16
ROWS = 16
WIDTH = 1024
PART = WIDTH // SLICES
SIDE = 128
BLOCKS = BATCH // SIDE
PACKED = BLOCKS * (BLOCKS + 1) // 2 * SIDE
CHUNK = PACKED // OWNERS
NT = (((1,), (1,)), ((), ()))
TN = (((0,), (0,)), ((), ()))


def swap(values, axes):
    return lax.all_to_all(values, axes, split_axis=0, concat_axis=0)


def place(i, j):
    return (i * (i + 1) // 2 + j) * SIDE


def call(kernel, out_shape, flops, *operands, scratch=(), scalars=0):
    moved = sum(o.size * o.dtype.itemsize for o in operands)
    specs = [pl.BlockSpec(memory_space=pltpu.SMEM)] * scalars
    specs += [pl.BlockSpec(memory_space=pltpu.VMEM)] * (len(operands) - scalars)
    many = isinstance(out_shape, (list, tuple))
    whole = pl.BlockSpec(memory_space=pltpu.VMEM)
    return pl.pallas_call(
        kernel,
        out_shape=out_shape,
        in_specs=specs,
        out_specs=[whole] * len(out_shape) if many else whole,
        scratch_shapes=list(scratch),
        cost_estimate=pl.CostEstimate(flops=flops, bytes_accessed=moved, transcendentals=0),
        compiler_params=pltpu.CompilerParams(vmem_limit_bytes=16 * 1024 * 1024),
    )(*operands)


def spread_kernel(one_ref, two_ref, out_ref, held_ref, sems):
    refs = (one_ref, two_ref)
    copies = [pltpu.make_async_copy(refs[v], held_ref.at[v], sems.at[v]) for v in range(2)]
    for copy in copies:
        copy.start()
    for v in range(2):
        copies[v].wait()
        for k in range(SLICES):
            piece = held_ref[v, :, k * PART : (k + 1) * PART]
            for h in range(GROUPS):
                out_ref[(h * SLICES + k) * 2 + 1 - v] = piece


def normalize(values):
    values = values.astype(jnp.float32)
    center = jnp.sum(values, axis=0, keepdims=True) / BATCH
    shifted = values - center
    spread = jnp.sum(shifted * shifted, axis=0, keepdims=True) / BATCH
    scaling = lax.rsqrt(spread + EPSILON)
    return (shifted * scaling).astype(jnp.bfloat16), scaling


def gram_kernel(raw_ref, other_ref, packed_ref):
    other_ref[...], _ = normalize(raw_ref[...])
    row = lax.broadcasted_iota(jnp.int32, (SIDE, SIDE), 0)
    column = lax.broadcasted_iota(jnp.int32, (SIDE, SIDE), 1)
    mean_diag = jnp.where(row == column, float(PART), 0.0)
    for i in range(BLOCKS):
        left = other_ref[i * SIDE : (i + 1) * SIDE]
        for j in range(i + 1):
            right = other_ref[j * SIDE : (j + 1) * SIDE]
            block = lax.dot_general(left, right, NT, preferred_element_type=jnp.float32)
            if i == j:
                block = block - mean_diag
            packed_ref[place(i, j) : place(i, j) + SIDE] = block.astype(jnp.bfloat16)


def mine_kernel(raw_ref, other_ref, mine_ref, terms_ref):
    mine_ref[...], scaling = normalize(raw_ref[...])
    both = mine_ref[...].astype(jnp.float32) * other_ref[...].astype(jnp.float32)
    on_diag = jnp.sum(both, axis=0, keepdims=True) / BATCH
    terms_ref[0:1] = scaling
    terms_ref[1:2] = on_diag
    terms_ref[2:3] = -2.0 * (1.0 - on_diag) - 2.0 * LAMBDA * on_diag


def sum_kernel(parts_ref, out_ref):
    total = parts_ref[0].astype(jnp.float32)
    for k in range(1, parts_ref.shape[0]):
        total = total + parts_ref[k].astype(jnp.float32)
    total = total.astype(jnp.bfloat16)
    for k in range(out_ref.shape[0]):
        out_ref[k] = total


def apply_kernel(place_ref, packed_ref, mine_ref, other_ref, terms_ref, out_ref, up_ref):
    group = place_ref[0]
    mine = [mine_ref[i * SIDE : (i + 1) * SIDE] for i in range(BLOCKS)]
    scaling, on_diag, slope = terms_ref[0:1], terms_ref[1:2], terms_ref[2:3]
    zero = jnp.zeros((1, PART), jnp.float32)
    squares, first, second = zero, zero, zero
    for i in range(BLOCKS):
        held = mine[i].astype(jnp.float32)
        product = FEATURES * held
        for j in range(BLOCKS):
            if i >= j:
                block = packed_ref[place(i, j) : place(i, j) + SIDE]
                product = product + jnp.dot(block, mine[j], preferred_element_type=jnp.float32)
            else:
                block = packed_ref[place(j, i) : place(j, i) + SIDE]
                product = product + lax.dot_general(
                    block, mine[j], TN, preferred_element_type=jnp.float32
                )
        other = other_ref[i * SIDE : (i + 1) * SIDE].astype(jnp.float32)
        up = (2.0 * LAMBDA / BATCH) * product + slope * other
        up_ref[i * SIDE : (i + 1) * SIDE] = up
        squares = squares + jnp.sum(product * held, axis=0, keepdims=True)
        first = first + jnp.sum(up, axis=0, keepdims=True)
        second = second + jnp.sum(up * held, axis=0, keepdims=True)
    squares, first, second = squares / (BATCH * BATCH), first / BATCH, second / BATCH
    loss = (1.0 - on_diag) * (1.0 - on_diag) + LAMBDA * (squares - on_diag * on_diag)
    for k in range(SLICES):
        for c in range(2):
            start = ((group * SLICES + k) * 2 + c) * ROWS
            rows = pl.ds(pl.multiple_of(start, ROWS), ROWS)
            held = mine_ref[rows].astype(jnp.float32)
            grad = scaling * (up_ref[rows] - first - held * second)
            out_ref[2 * k + c, :, :PART] = grad.astype(jnp.bfloat16)
    high = loss.astype(jnp.bfloat16)
    rest = loss - high.astype(jnp.float32)
    middle = rest.astype(jnp.bfloat16)
    low = (rest - middle.astype(jnp.float32)).astype(jnp.bfloat16)
    index = lax.broadcasted_iota(jnp.int32, (ROWS, SIDE), 0)
    tail = jnp.zeros((ROWS, SIDE), jnp.float32)
    for n, term in enumerate((high, middle, low)):
        for half in range(PART // SIDE):
            row = term[:, half * SIDE : (half + 1) * SIDE].astype(jnp.float32)
            tail = jnp.where(index == n * (PART // SIDE) + half, row, tail)
    tail = tail.astype(jnp.bfloat16)
    for k in range(2 * SLICES):
        out_ref[k, :, PART:] = tail


def unpack_kernel(parts_ref, loss_ref, one_ref, two_ref):
    halves = PART // SIDE
    for k in range(SLICES):
        columns = slice(k * PART, (k + 1) * PART)
        one_ref[:, columns] = parts_ref[2 * k, :, :PART].astype(jnp.float32)
        two_ref[:, columns] = parts_ref[2 * k + 1, :, :PART].astype(jnp.float32)
        tail = parts_ref[2 * k, :, PART:].astype(jnp.float32)
        for half in range(halves):
            high, middle, low = [tail[n * halves + half : n * halves + half + 1] for n in range(3)]
            start = k * PART + half * SIDE
            loss_ref[:, start : start + SIDE] = high + (middle + low)


def local(view_one, view_two):
    bf16, f32 = jnp.bfloat16, jnp.float32
    shape = jax.ShapeDtypeStruct
    group = lax.axis_index("zh").astype(jnp.int32).reshape(1)

    sent = pl.pallas_call(
        spread_kernel,
        out_shape=pltpu.VMEM((2 * OWNERS, ROWS, PART), bf16),
        in_specs=[pl.BlockSpec(memory_space=pl.ANY)] * 2,
        out_specs=pl.BlockSpec(memory_space=pltpu.VMEM),
        scratch_shapes=[pltpu.VMEM((2, ROWS, WIDTH), bf16), pltpu.SemaphoreType.DMA((2,))],
    )(view_one, view_two)
    raw = swap(sent, IMAGES).reshape(BATCH, PART)
    raw_mine = lax.ppermute(raw, "c", [(0, 1), (1, 0)])

    other, packed = call(
        gram_kernel,
        [shape((BATCH, PART), bf16), shape((PACKED, SIDE), bf16)],
        2 * BATCH * BATCH * PART,
        raw,
    )
    mine, terms = call(
        mine_kernel, [shape((BATCH, PART), bf16), shape((8, PART), f32)], 0, raw_mine, other
    )
    strips = swap(packed.reshape(OWNERS, CHUNK, SIDE), FEAT)
    strips = swap(call(sum_kernel, shape((SLICES, CHUNK, SIDE), bf16), 0, strips), "zl")
    strips = swap(call(sum_kernel, shape((OWNERS, CHUNK, SIDE), bf16), 0, strips), FEAT)

    out = call(
        apply_kernel,
        shape((2 * SLICES, ROWS, PART + SIDE), bf16),
        2 * BATCH * BATCH * PART,
        group,
        strips.reshape(PACKED, SIDE),
        mine,
        other,
        terms,
        scratch=[pltpu.VMEM((BATCH, PART), f32)],
        scalars=1,
    )
    loss, one, two = call(
        unpack_kernel,
        [shape((1, WIDTH), f32), shape((ROWS, WIDTH), f32), shape((ROWS, WIDTH), f32)],
        0,
        swap(out, ("zl", "c")),
    )
    return (loss.reshape(WIDTH), one, two)


def solution(mesh):
    cut = Mesh(mesh.devices.reshape(CUTS), NAMES)
    spread = P(IMAGES, FEAT)
    return jax.shard_map(
        local, mesh=cut, in_specs=(spread, spread), out_specs=(P(FEAT), spread, spread), check_vma=False
    )
```

```python
import jax
import jax.numpy as jnp
from jax import lax
from jax.experimental import pallas as pl
from jax.experimental.pallas import tpu as pltpu
from jax.sharding import Mesh, PartitionSpec as P

EPSILON = 1e-05
LAMBDA = 0.0051
FEATURES = 16384
BATCH = 512

CUTS = (2, 2, 2, 2, 2, 4, 4)
NAMES = ("a", "b", "e", "d", "c", "y", "x")
IMAGES = ('b', 'e', 'd', 'a', 'c')
NEAR = ("e", "d")
FEAT = ("y", "x")
GROUPS = 4
SLICES = 4
OWNERS = 16
ROWS = 16
WIDTH = 1024
PART = WIDTH // SLICES
SIDE = 128
BLOCKS = BATCH // SIDE
PACKED = BLOCKS * (BLOCKS + 1) // 2 * SIDE
CHUNK = PACKED // OWNERS
NT = (((1,), (1,)), ((), ()))
TN = (((0,), (0,)), ((), ()))


def swap(values, axes):
    return lax.all_to_all(values, axes, split_axis=0, concat_axis=0)


def place(i, j):
    return (i * (i + 1) // 2 + j) * SIDE


def call(kernel, out_shape, flops, *operands, scratch=(), scalars=0):
    moved = sum(o.size * o.dtype.itemsize for o in operands)
    specs = [pl.BlockSpec(memory_space=pltpu.SMEM)] * scalars
    specs += [pl.BlockSpec(memory_space=pltpu.VMEM)] * (len(operands) - scalars)
    many = isinstance(out_shape, (list, tuple))
    whole = pl.BlockSpec(memory_space=pltpu.VMEM)
    return pl.pallas_call(
        kernel,
        out_shape=out_shape,
        in_specs=specs,
        out_specs=[whole] * len(out_shape) if many else whole,
        scratch_shapes=list(scratch),
        cost_estimate=pl.CostEstimate(flops=flops, bytes_accessed=moved, transcendentals=0),
        compiler_params=pltpu.CompilerParams(vmem_limit_bytes=16 * 1024 * 1024),
    )(*operands)


def position(h, k, c):
    return (h % 2) * 16 + (k // 2) * 8 + (k % 2) * 4 + (h // 2) * 2 + (c) * 1


def spread_kernel(one_ref, two_ref, out_ref, held_ref, sems):
    refs = (one_ref, two_ref)
    copies = [pltpu.make_async_copy(refs[v], held_ref.at[v], sems.at[v]) for v in range(2)]
    for copy in copies:
        copy.start()
    for v in range(2):
        copies[v].wait()
        for k in range(SLICES):
            piece = held_ref[v, :, k * PART : (k + 1) * PART]
            for h in range(GROUPS):
                out_ref[position(h, k, 1 - v)] = piece


def normalize(values):
    values = values.astype(jnp.float32)
    center = jnp.sum(values, axis=0, keepdims=True) / BATCH
    shifted = values - center
    spread = jnp.sum(shifted * shifted, axis=0, keepdims=True) / BATCH
    scaling = lax.rsqrt(spread + EPSILON)
    return (shifted * scaling).astype(jnp.bfloat16), scaling


def gram_kernel(raw_ref, other_ref, packed_ref):
    other_ref[...], _ = normalize(raw_ref[...])
    row = lax.broadcasted_iota(jnp.int32, (SIDE, SIDE), 0)
    column = lax.broadcasted_iota(jnp.int32, (SIDE, SIDE), 1)
    mean_diag = jnp.where(row == column, float(PART), 0.0)
    for i in range(BLOCKS):
        left = other_ref[i * SIDE : (i + 1) * SIDE]
        for j in range(i + 1):
            right = other_ref[j * SIDE : (j + 1) * SIDE]
            block = lax.dot_general(left, right, NT, preferred_element_type=jnp.float32)
            if i == j:
                block = block - mean_diag
            packed_ref[place(i, j) : place(i, j) + SIDE] = block.astype(jnp.bfloat16)


def mine_kernel(raw_ref, other_ref, mine_ref, terms_ref):
    mine_ref[...], scaling = normalize(raw_ref[...])
    both = mine_ref[...].astype(jnp.float32) * other_ref[...].astype(jnp.float32)
    on_diag = jnp.sum(both, axis=0, keepdims=True) / BATCH
    terms_ref[0:1] = scaling
    terms_ref[1:2] = on_diag
    terms_ref[2:3] = -2.0 * (1.0 - on_diag) - 2.0 * LAMBDA * on_diag


def sum_kernel(parts_ref, out_ref):
    total = parts_ref[0].astype(jnp.float32)
    for k in range(1, parts_ref.shape[0]):
        total = total + parts_ref[k].astype(jnp.float32)
    total = total.astype(jnp.bfloat16)
    for k in range(out_ref.shape[0]):
        out_ref[k] = total


def apply_kernel(place_ref, packed_ref, mine_ref, other_ref, terms_ref, out_ref, up_ref):
    group = place_ref[0]
    mine = [mine_ref[i * SIDE : (i + 1) * SIDE] for i in range(BLOCKS)]
    scaling, on_diag, slope = terms_ref[0:1], terms_ref[1:2], terms_ref[2:3]
    zero = jnp.zeros((1, PART), jnp.float32)
    squares, first, second = zero, zero, zero
    for i in range(BLOCKS):
        held = mine[i].astype(jnp.float32)
        product = FEATURES * held
        for j in range(BLOCKS):
            if i >= j:
                block = packed_ref[place(i, j) : place(i, j) + SIDE]
                product = product + jnp.dot(block, mine[j], preferred_element_type=jnp.float32)
            else:
                block = packed_ref[place(j, i) : place(j, i) + SIDE]
                product = product + lax.dot_general(
                    block, mine[j], TN, preferred_element_type=jnp.float32
                )
        other = other_ref[i * SIDE : (i + 1) * SIDE].astype(jnp.float32)
        up = (2.0 * LAMBDA / BATCH) * product + slope * other
        up_ref[i * SIDE : (i + 1) * SIDE] = up
        squares = squares + jnp.sum(product * held, axis=0, keepdims=True)
        first = first + jnp.sum(up, axis=0, keepdims=True)
        second = second + jnp.sum(up * held, axis=0, keepdims=True)
    squares, first, second = squares / (BATCH * BATCH), first / BATCH, second / BATCH
    loss = (1.0 - on_diag) * (1.0 - on_diag) + LAMBDA * (squares - on_diag * on_diag)
    for k in range(SLICES):
        for c in range(2):
            start = position(group, k, c) * ROWS
            rows = pl.ds(pl.multiple_of(start, ROWS), ROWS)
            held = mine_ref[rows].astype(jnp.float32)
            grad = scaling * (up_ref[rows] - first - held * second)
            out_ref[2 * k + c, :, :PART] = grad.astype(jnp.bfloat16)
    high = loss.astype(jnp.bfloat16)
    rest = loss - high.astype(jnp.float32)
    middle = rest.astype(jnp.bfloat16)
    low = (rest - middle.astype(jnp.float32)).astype(jnp.bfloat16)
    index = lax.broadcasted_iota(jnp.int32, (ROWS, SIDE), 0)
    tail = jnp.zeros((ROWS, SIDE), jnp.float32)
    for n, term in enumerate((high, middle, low)):
        for half in range(PART // SIDE):
            row = term[:, half * SIDE : (half + 1) * SIDE].astype(jnp.float32)
            tail = jnp.where(index == n * (PART // SIDE) + half, row, tail)
    tail = tail.astype(jnp.bfloat16)
    for k in range(2 * SLICES):
        out_ref[k, :, PART:] = tail


def unpack_kernel(parts_ref, loss_ref, one_ref, two_ref):
    halves = PART // SIDE
    for k in range(SLICES):
        columns = slice(k * PART, (k + 1) * PART)
        one_ref[:, columns] = parts_ref[2 * k, :, :PART].astype(jnp.float32)
        two_ref[:, columns] = parts_ref[2 * k + 1, :, :PART].astype(jnp.float32)
        tail = parts_ref[2 * k, :, PART:].astype(jnp.float32)
        for half in range(halves):
            high, middle, low = [tail[n * halves + half : n * halves + half + 1] for n in range(3)]
            start = k * PART + half * SIDE
            loss_ref[:, start : start + SIDE] = high + (middle + low)


def local(view_one, view_two):
    bf16, f32 = jnp.bfloat16, jnp.float32
    shape = jax.ShapeDtypeStruct
    group = (lax.axis_index("a") * 2 + lax.axis_index("b")).astype(jnp.int32).reshape(1)

    sent = pl.pallas_call(
        spread_kernel,
        out_shape=pltpu.VMEM((2 * OWNERS, ROWS, PART), bf16),
        in_specs=[pl.BlockSpec(memory_space=pl.ANY)] * 2,
        out_specs=pl.BlockSpec(memory_space=pltpu.VMEM),
        scratch_shapes=[pltpu.VMEM((2, ROWS, WIDTH), bf16), pltpu.SemaphoreType.DMA((2,))],
    )(view_one, view_two)
    raw = swap(sent, IMAGES).reshape(BATCH, PART)
    raw_mine = lax.ppermute(raw, "c", [(0, 1), (1, 0)])

    other, packed = call(
        gram_kernel,
        [shape((BATCH, PART), bf16), shape((PACKED, SIDE), bf16)],
        2 * BATCH * BATCH * PART,
        raw,
    )
    mine, terms = call(
        mine_kernel, [shape((BATCH, PART), bf16), shape((8, PART), f32)], 0, raw_mine, other
    )
    strips = swap(packed.reshape(OWNERS, CHUNK, SIDE), FEAT)
    strips = swap(call(sum_kernel, shape((SLICES, CHUNK, SIDE), bf16), 0, strips), ("d", "e"))
    strips = swap(call(sum_kernel, shape((OWNERS, CHUNK, SIDE), bf16), 0, strips), FEAT)

    out = call(
        apply_kernel,
        shape((2 * SLICES, ROWS, PART + SIDE), bf16),
        2 * BATCH * BATCH * PART,
        group,
        strips.reshape(PACKED, SIDE),
        mine,
        other,
        terms,
        scratch=[pltpu.VMEM((BATCH, PART), f32)],
        scalars=1,
    )
    loss, one, two = call(
        unpack_kernel,
        [shape((1, WIDTH), f32), shape((ROWS, WIDTH), f32), shape((ROWS, WIDTH), f32)],
        0,
        swap(out, ("e", "d", "c")),
    )
    return (loss.reshape(WIDTH), one, two)


def solution(mesh):
    cut = Mesh(mesh.devices.reshape(CUTS), NAMES)
    spread = P(NAMES[:5], FEAT)
    return jax.shard_map(
        local, mesh=cut, in_specs=(spread, spread), out_specs=(P(FEAT), spread, spread), check_vma=False
    )
```

```python
import jax
import jax.numpy as jnp
from jax import lax
from jax.experimental import pallas as pl
from jax.experimental.pallas import tpu as pltpu
from jax.sharding import PartitionSpec as P

EPSILON = 1e-05
LAMBDA = 0.0051
FEATURES = 16384
BATCH = 512

CHIPS = (0, 4, 2, 6, 1, 5, 3, 7, 8, 12, 10, 14, 9, 13, 11, 15)
GROUPS = 4
SLICES = 4
OWNERS = 16
ROWS = 16
WIDTH = 1024
PART = WIDTH // SLICES
SIDE = 128
BLOCKS = BATCH // SIDE
PACKED = BLOCKS * (BLOCKS + 1) // 2 * SIDE
CHUNK = PACKED // OWNERS
NT = (((1,), (1,)), ((), ()))
TN = (((0,), (0,)), ((), ()))


SAME_CORE = [[2 * z + c for z in CHIPS] for c in range(2)]
CORES = [[2 * z, 2 * z + 1] for z in range(16)]
NEAR = [[8 * h + 2 * k + c for k in (0, 2, 1, 3)] for h in range(4) for c in range(2)]
GROUP = [list(range(8 * h, 8 * h + 8)) for h in range(4)]


def swap(values, axis, groups=None):
    return lax.all_to_all(values, axis, split_axis=0, concat_axis=0, axis_index_groups=groups)


def place(i, j):
    return (i * (i + 1) // 2 + j) * SIDE


def call(kernel, out_shape, flops, *operands, scratch=(), scalars=0):
    moved = sum(o.size * o.dtype.itemsize for o in operands)
    specs = [pl.BlockSpec(memory_space=pltpu.SMEM)] * scalars
    specs += [pl.BlockSpec(memory_space=pltpu.VMEM)] * (len(operands) - scalars)
    many = isinstance(out_shape, (list, tuple))
    whole = pl.BlockSpec(memory_space=pltpu.VMEM)
    return pl.pallas_call(
        kernel,
        out_shape=out_shape,
        in_specs=specs,
        out_specs=[whole] * len(out_shape) if many else whole,
        scratch_shapes=list(scratch),
        cost_estimate=pl.CostEstimate(flops=flops, bytes_accessed=moved, transcendentals=0),
        compiler_params=pltpu.CompilerParams(vmem_limit_bytes=16 * 1024 * 1024),
    )(*operands)


def spread_kernel(one_ref, two_ref, out_ref, held_ref, sems):
    refs = (one_ref, two_ref)
    copies = [pltpu.make_async_copy(refs[v], held_ref.at[v], sems.at[v]) for v in range(2)]
    for copy in copies:
        copy.start()
    for v in range(2):
        copies[v].wait()
        for k in range(SLICES):
            piece = held_ref[v, :, k * PART : (k + 1) * PART]
            for h in range(GROUPS):
                out_ref[CHIPS.index(h * SLICES + k), v] = piece


def normalize(values):
    values = values.astype(jnp.float32)
    center = jnp.sum(values, axis=0, keepdims=True) / BATCH
    shifted = values - center
    spread = jnp.sum(shifted * shifted, axis=0, keepdims=True) / BATCH
    scaling = lax.rsqrt(spread + EPSILON)
    return (shifted * scaling).astype(jnp.bfloat16), scaling


def gram_kernel(core_ref, whole_ref, mine_ref, other_ref, terms_ref, packed_ref):
    core = core_ref[0]
    other_ref[...], _ = normalize(whole_ref[:, :, 1 - core].reshape(BATCH, PART))
    row = lax.broadcasted_iota(jnp.int32, (SIDE, SIDE), 0)
    column = lax.broadcasted_iota(jnp.int32, (SIDE, SIDE), 1)
    mean_diag = jnp.where(row == column, float(PART), 0.0)
    for i in range(BLOCKS):
        left = other_ref[i * SIDE : (i + 1) * SIDE]
        for j in range(i + 1):
            right = other_ref[j * SIDE : (j + 1) * SIDE]
            block = lax.dot_general(left, right, NT, preferred_element_type=jnp.float32)
            if i == j:
                block = block - mean_diag
            packed_ref[place(i, j) : place(i, j) + SIDE] = block.astype(jnp.bfloat16)
    mine_ref[...], scaling = normalize(whole_ref[:, :, core].reshape(BATCH, PART))
    both = mine_ref[...].astype(jnp.float32) * other_ref[...].astype(jnp.float32)
    on_diag = jnp.sum(both, axis=0, keepdims=True) / BATCH
    terms_ref[0:1] = scaling
    terms_ref[1:2] = on_diag
    terms_ref[2:3] = -2.0 * (1.0 - on_diag) - 2.0 * LAMBDA * on_diag


def sum_kernel(parts_ref, out_ref):
    total = parts_ref[0].astype(jnp.float32)
    for k in range(1, parts_ref.shape[0]):
        total = total + parts_ref[k].astype(jnp.float32)
    total = total.astype(jnp.bfloat16)
    for k in range(out_ref.shape[0]):
        out_ref[k] = total


def apply_kernel(place_ref, packed_ref, mine_ref, other_ref, terms_ref, out_ref, up_ref):
    group = place_ref[0]
    mine = [mine_ref[i * SIDE : (i + 1) * SIDE] for i in range(BLOCKS)]
    scaling, on_diag, slope = terms_ref[0:1], terms_ref[1:2], terms_ref[2:3]
    zero = jnp.zeros((1, PART), jnp.float32)
    squares, first, second = zero, zero, zero
    for i in range(BLOCKS):
        held = mine[i].astype(jnp.float32)
        product = FEATURES * held
        for j in range(BLOCKS):
            if i >= j:
                block = packed_ref[place(i, j) : place(i, j) + SIDE]
                product = product + jnp.dot(block, mine[j], preferred_element_type=jnp.float32)
            else:
                block = packed_ref[place(j, i) : place(j, i) + SIDE]
                product = product + lax.dot_general(
                    block, mine[j], TN, preferred_element_type=jnp.float32
                )
        other = other_ref[i * SIDE : (i + 1) * SIDE].astype(jnp.float32)
        up = (2.0 * LAMBDA / BATCH) * product + slope * other
        up_ref[i * SIDE : (i + 1) * SIDE] = up
        squares = squares + jnp.sum(product * held, axis=0, keepdims=True)
        first = first + jnp.sum(up, axis=0, keepdims=True)
        second = second + jnp.sum(up * held, axis=0, keepdims=True)
    squares, first, second = squares / (BATCH * BATCH), first / BATCH, second / BATCH
    loss = (1.0 - on_diag) * (1.0 - on_diag) + LAMBDA * (squares - on_diag * on_diag)
    for k in range(SLICES):
        places = [CHIPS.index(h * SLICES + k) for h in range(GROUPS)]
        order = sum(jnp.where(group == h, places[h], 0) for h in range(GROUPS))
        for c in range(2):
            start = c * (BATCH // 2) + order * ROWS
            rows = pl.ds(pl.multiple_of(start, ROWS), ROWS)
            held = mine_ref[rows].astype(jnp.float32)
            grad = scaling * (up_ref[rows] - first - held * second)
            out_ref[2 * k + c, :, :PART] = grad.astype(jnp.bfloat16)
    high = loss.astype(jnp.bfloat16)
    rest = loss - high.astype(jnp.float32)
    middle = rest.astype(jnp.bfloat16)
    low = (rest - middle.astype(jnp.float32)).astype(jnp.bfloat16)
    index = lax.broadcasted_iota(jnp.int32, (ROWS, SIDE), 0)
    tail = jnp.zeros((ROWS, SIDE), jnp.float32)
    for n, term in enumerate((high, middle, low)):
        for half in range(PART // SIDE):
            row = term[:, half * SIDE : (half + 1) * SIDE].astype(jnp.float32)
            tail = jnp.where(index == n * (PART // SIDE) + half, row, tail)
    tail = tail.astype(jnp.bfloat16)
    for k in range(2 * SLICES):
        out_ref[k, :, PART:] = tail


def unpack_kernel(parts_ref, loss_ref, one_ref, two_ref):
    halves = PART // SIDE
    for k in range(SLICES):
        columns = slice(k * PART, (k + 1) * PART)
        one_ref[:, columns] = parts_ref[2 * k, :, :PART].astype(jnp.float32)
        two_ref[:, columns] = parts_ref[2 * k + 1, :, :PART].astype(jnp.float32)
        tail = parts_ref[2 * k, :, PART:].astype(jnp.float32)
        for half in range(halves):
            high, middle, low = [tail[n * halves + half : n * halves + half + 1] for n in range(3)]
            start = k * PART + half * SIDE
            loss_ref[:, start : start + SIDE] = high + (middle + low)


def local(view_one, view_two):
    bf16, f32 = jnp.bfloat16, jnp.float32
    shape = jax.ShapeDtypeStruct
    device = lax.axis_index("batch").astype(jnp.int32).reshape(1)
    core, group = device % 2, device // 8

    sent = pl.pallas_call(
        spread_kernel,
        out_shape=pltpu.VMEM((OWNERS, 2, ROWS, PART), bf16),
        in_specs=[pl.BlockSpec(memory_space=pl.ANY)] * 2,
        out_specs=pl.BlockSpec(memory_space=pltpu.VMEM),
        scratch_shapes=[pltpu.VMEM((2, ROWS, WIDTH), bf16), pltpu.SemaphoreType.DMA((2,))],
    )(view_one, view_two)
    sent, core, group = lax.optimization_barrier((sent, core, group))
    whole = lax.all_gather(swap(sent, "batch", SAME_CORE), "batch", axis_index_groups=CORES)

    mine, other, terms, packed = call(
        gram_kernel,
        [
            pltpu.VMEM((BATCH, PART), bf16),
            pltpu.VMEM((BATCH, PART), bf16),
            pltpu.VMEM((8, PART), f32),
            pltpu.VMEM((PACKED, SIDE), bf16),
        ],
        2 * BATCH * BATCH * PART,
        core,
        whole,
        scalars=1,
    )
    strips = swap(packed.reshape(OWNERS, CHUNK, SIDE), "feat")
    strips = swap(call(sum_kernel, shape((SLICES, CHUNK, SIDE), bf16), 0, strips), "batch", NEAR)
    strips = swap(call(sum_kernel, shape((OWNERS, CHUNK, SIDE), bf16), 0, strips), "feat")

    out = call(
        apply_kernel,
        shape((2 * SLICES, ROWS, PART + SIDE), bf16),
        2 * BATCH * BATCH * PART,
        group,
        strips.reshape(PACKED, SIDE),
        mine,
        other,
        terms,
        scratch=[pltpu.VMEM((BATCH, PART), f32)],
        scalars=1,
    )
    loss, one, two = call(
        unpack_kernel,
        [shape((1, WIDTH), f32), shape((ROWS, WIDTH), f32), shape((ROWS, WIDTH), f32)],
        0,
        swap(out, "batch", GROUP),
    )
    return (loss.reshape(WIDTH), one, two)


def solution(mesh):
    spread = P("batch", "feat")
    return jax.shard_map(
        local, mesh=mesh, in_specs=(spread, spread), out_specs=(P("feat"), spread, spread), check_vma=False
    )
```

```python
import jax
import jax.numpy as jnp
from jax import lax
from jax.experimental import pallas as pl
from jax.experimental.pallas import tpu as pltpu
from jax.sharding import PartitionSpec as P

EPSILON = 1e-05
LAMBDA = 0.0051
FEATURES = 16384
BATCH = 512

CHIPS = (8, 7, 9, 6, 10, 5, 11, 4, 12, 3, 13, 2, 14, 1, 15, 0)
NEAR = (1, 2, 0, 3)
OWNER = (2, 3, 4, 5, 0, 1, 6, 7)
FEAT = (5, 6, 9, 10, 4, 7, 1, 2, 8, 11, 13, 14, 0, 3, 12, 15)
GROUPS = 4
SLICES = 4
OWNERS = 16
ROWS = 16
WIDTH = 1024
PART = WIDTH // SLICES
SIDE = 128
BLOCKS = BATCH // SIDE
PACKED = BLOCKS * (BLOCKS + 1) // 2 * SIDE
CHUNK = PACKED // OWNERS
NT = (((1,), (1,)), ((), ()))
TN = (((0,), (0,)), ((), ()))


SAME_CORE = [[2 * z + c for z in CHIPS] for c in range(2)]
CORES = [[2 * z, 2 * z + 1] for z in range(16)]
NEIGHBOURS = [[8 * h + 2 * k + c for k in NEAR] for h in range(4) for c in range(2)]
GROUP = [[8 * h + i for i in OWNER] for h in range(4)]


def swap(values, axis, groups=None):
    return lax.all_to_all(values, axis, split_axis=0, concat_axis=0, axis_index_groups=groups)


def place(i, j):
    return (i * (i + 1) // 2 + j) * SIDE


def call(kernel, out_shape, flops, *operands, scratch=(), scalars=0):
    moved = sum(o.size * o.dtype.itemsize for o in operands)
    specs = [pl.BlockSpec(memory_space=pltpu.SMEM)] * scalars
    specs += [pl.BlockSpec(memory_space=pltpu.VMEM)] * (len(operands) - scalars)
    many = isinstance(out_shape, (list, tuple))
    whole = pl.BlockSpec(memory_space=pltpu.VMEM)
    return pl.pallas_call(
        kernel,
        out_shape=out_shape,
        in_specs=specs,
        out_specs=[whole] * len(out_shape) if many else whole,
        scratch_shapes=list(scratch),
        cost_estimate=pl.CostEstimate(flops=flops, bytes_accessed=moved, transcendentals=0),
        compiler_params=pltpu.CompilerParams(vmem_limit_bytes=16 * 1024 * 1024),
    )(*operands)


def spread_kernel(one_ref, two_ref, out_ref, held_ref, sems):
    refs = (one_ref, two_ref)
    copies = [pltpu.make_async_copy(refs[v], held_ref.at[v], sems.at[v]) for v in range(2)]
    for copy in copies:
        copy.start()
    for v in range(2):
        copies[v].wait()
        for k in range(SLICES):
            piece = held_ref[v, :, k * PART : (k + 1) * PART]
            for h in range(GROUPS):
                out_ref[CHIPS.index(h * SLICES + k), v] = piece


def normalize(values):
    values = values.astype(jnp.float32)
    center = jnp.sum(values, axis=0, keepdims=True) / BATCH
    shifted = values - center
    spread = jnp.sum(shifted * shifted, axis=0, keepdims=True) / BATCH
    scaling = lax.rsqrt(spread + EPSILON)
    return (shifted * scaling).astype(jnp.bfloat16), scaling


def gram_kernel(core_ref, whole_ref, mine_ref, other_ref, terms_ref, packed_ref):
    core = core_ref[0]
    other_ref[...], _ = normalize(whole_ref[:, :, 1 - core].reshape(BATCH, PART))
    row = lax.broadcasted_iota(jnp.int32, (SIDE, SIDE), 0)
    column = lax.broadcasted_iota(jnp.int32, (SIDE, SIDE), 1)
    mean_diag = jnp.where(row == column, float(PART), 0.0)
    for i in range(BLOCKS):
        left = other_ref[i * SIDE : (i + 1) * SIDE]
        for j in range(i + 1):
            right = other_ref[j * SIDE : (j + 1) * SIDE]
            block = lax.dot_general(left, right, NT, preferred_element_type=jnp.float32)
            if i == j:
                block = block - mean_diag
            packed_ref[place(i, j) : place(i, j) + SIDE] = block.astype(jnp.bfloat16)
    mine_ref[...], scaling = normalize(whole_ref[:, :, core].reshape(BATCH, PART))
    both = mine_ref[...].astype(jnp.float32) * other_ref[...].astype(jnp.float32)
    on_diag = jnp.sum(both, axis=0, keepdims=True) / BATCH
    terms_ref[0:1] = scaling
    terms_ref[1:2] = on_diag
    terms_ref[2:3] = -2.0 * (1.0 - on_diag) - 2.0 * LAMBDA * on_diag


def sum_kernel(parts_ref, out_ref):
    total = parts_ref[0].astype(jnp.float32)
    for k in range(1, parts_ref.shape[0]):
        total = total + parts_ref[k].astype(jnp.float32)
    total = total.astype(jnp.bfloat16)
    for k in range(out_ref.shape[0]):
        out_ref[k] = total


def apply_kernel(place_ref, packed_ref, mine_ref, other_ref, terms_ref, out_ref, up_ref):
    group = place_ref[0]
    mine = [mine_ref[i * SIDE : (i + 1) * SIDE] for i in range(BLOCKS)]
    scaling, on_diag, slope = terms_ref[0:1], terms_ref[1:2], terms_ref[2:3]
    zero = jnp.zeros((1, PART), jnp.float32)
    squares, first, second = zero, zero, zero
    for i in range(BLOCKS):
        held = mine[i].astype(jnp.float32)
        product = FEATURES * held
        for j in range(BLOCKS):
            if i >= j:
                block = packed_ref[place(i, j) : place(i, j) + SIDE]
                product = product + jnp.dot(block, mine[j], preferred_element_type=jnp.float32)
            else:
                block = packed_ref[place(j, i) : place(j, i) + SIDE]
                product = product + lax.dot_general(
                    block, mine[j], TN, preferred_element_type=jnp.float32
                )
        other = other_ref[i * SIDE : (i + 1) * SIDE].astype(jnp.float32)
        up = (2.0 * LAMBDA / BATCH) * product + slope * other
        up_ref[i * SIDE : (i + 1) * SIDE] = up
        squares = squares + jnp.sum(product * held, axis=0, keepdims=True)
        first = first + jnp.sum(up, axis=0, keepdims=True)
        second = second + jnp.sum(up * held, axis=0, keepdims=True)
    squares, first, second = squares / (BATCH * BATCH), first / BATCH, second / BATCH
    loss = (1.0 - on_diag) * (1.0 - on_diag) + LAMBDA * (squares - on_diag * on_diag)
    for k in range(SLICES):
        places = [CHIPS.index(h * SLICES + k) for h in range(GROUPS)]
        order = sum(jnp.where(group == h, places[h], 0) for h in range(GROUPS))
        for c in range(2):
            start = c * (BATCH // 2) + order * ROWS
            rows = pl.ds(pl.multiple_of(start, ROWS), ROWS)
            held = mine_ref[rows].astype(jnp.float32)
            grad = scaling * (up_ref[rows] - first - held * second)
            out_ref[OWNER.index(2 * k + c), :, :PART] = grad.astype(jnp.bfloat16)
    high = loss.astype(jnp.bfloat16)
    rest = loss - high.astype(jnp.float32)
    middle = rest.astype(jnp.bfloat16)
    low = (rest - middle.astype(jnp.float32)).astype(jnp.bfloat16)
    index = lax.broadcasted_iota(jnp.int32, (ROWS, SIDE), 0)
    tail = jnp.zeros((ROWS, SIDE), jnp.float32)
    for n, term in enumerate((high, middle, low)):
        for half in range(PART // SIDE):
            row = term[:, half * SIDE : (half + 1) * SIDE].astype(jnp.float32)
            tail = jnp.where(index == n * (PART // SIDE) + half, row, tail)
    tail = tail.astype(jnp.bfloat16)
    for k in range(2 * SLICES):
        out_ref[k, :, PART:] = tail


def unpack_kernel(parts_ref, loss_ref, one_ref, two_ref):
    halves = PART // SIDE
    for k in range(SLICES):
        columns = slice(k * PART, (k + 1) * PART)
        one_ref[:, columns] = parts_ref[OWNER.index(2 * k), :, :PART].astype(jnp.float32)
        two_ref[:, columns] = parts_ref[OWNER.index(2 * k + 1), :, :PART].astype(jnp.float32)
        tail = parts_ref[OWNER.index(2 * k), :, PART:].astype(jnp.float32)
        for half in range(halves):
            high, middle, low = [tail[n * halves + half : n * halves + half + 1] for n in range(3)]
            start = k * PART + half * SIDE
            loss_ref[:, start : start + SIDE] = high + (middle + low)


def local(view_one, view_two):
    bf16, f32 = jnp.bfloat16, jnp.float32
    shape = jax.ShapeDtypeStruct
    device = lax.axis_index("batch").astype(jnp.int32).reshape(1)
    core, group = device % 2, device // 8

    sent = pl.pallas_call(
        spread_kernel,
        out_shape=pltpu.VMEM((OWNERS, 2, ROWS, PART), bf16),
        in_specs=[pl.BlockSpec(memory_space=pl.ANY)] * 2,
        out_specs=pl.BlockSpec(memory_space=pltpu.VMEM),
        scratch_shapes=[pltpu.VMEM((2, ROWS, WIDTH), bf16), pltpu.SemaphoreType.DMA((2,))],
    )(view_one, view_two)
    sent, core, group = lax.optimization_barrier((sent, core, group))
    whole = lax.all_gather(swap(sent, "batch", SAME_CORE), "batch", axis_index_groups=CORES)

    mine, other, terms, packed = call(
        gram_kernel,
        [
            pltpu.VMEM((BATCH, PART), bf16),
            pltpu.VMEM((BATCH, PART), bf16),
            pltpu.VMEM((8, PART), f32),
            pltpu.VMEM((PACKED, SIDE), bf16),
        ],
        2 * BATCH * BATCH * PART,
        core,
        whole,
        scalars=1,
    )
    strips = swap(packed.reshape(OWNERS, CHUNK, SIDE), "feat", [list(FEAT)])
    strips = swap(call(sum_kernel, shape((SLICES, CHUNK, SIDE), bf16), 0, strips), "batch", NEIGHBOURS)
    strips = swap(call(sum_kernel, shape((OWNERS, CHUNK, SIDE), bf16), 0, strips), "feat", [list(FEAT)])

    out = call(
        apply_kernel,
        shape((2 * SLICES, ROWS, PART + SIDE), bf16),
        2 * BATCH * BATCH * PART,
        group,
        strips.reshape(PACKED, SIDE),
        mine,
        other,
        terms,
        scratch=[pltpu.VMEM((BATCH, PART), f32)],
        scalars=1,
    )
    loss, one, two = call(
        unpack_kernel,
        [shape((1, WIDTH), f32), shape((ROWS, WIDTH), f32), shape((ROWS, WIDTH), f32)],
        0,
        swap(out, "batch", GROUP),
    )
    return (loss.reshape(WIDTH), one, two)


def solution(mesh):
    spread = P("batch", "feat")
    return jax.shard_map(
        local, mesh=mesh, in_specs=(spread, spread), out_specs=(P("feat"), spread, spread), check_vma=False
    )
```

```python
import jax
import jax.numpy as jnp
from jax import lax
from jax.experimental import pallas as pl
from jax.experimental.pallas import tpu as pltpu
from jax.sharding import PartitionSpec as P

EPSILON = 1e-05
LAMBDA = 0.0051
FEATURES = 16384
BATCH = 512

CHIPS = (10, 9, 11, 8, 12, 7, 13, 6, 14, 5, 15, 4, 3, 2, 1, 0)
NEAR = (1, 2, 0, 3)
OWNER = (2, 3, 4, 5, 0, 1, 6, 7)
FEAT = (10, 11, 12, 13, 14, 15, 0, 1, 2, 3, 4, 5, 6, 7, 8, 9)
GROUPS = 4
SLICES = 4
OWNERS = 16
ROWS = 16
WIDTH = 1024
PART = WIDTH // SLICES
SIDE = 128
BLOCKS = BATCH // SIDE
PACKED = BLOCKS * (BLOCKS + 1) // 2 * SIDE
CHUNK = PACKED // OWNERS
NT = (((1,), (1,)), ((), ()))
TN = (((0,), (0,)), ((), ()))


SAME_CORE = [[2 * z + c for z in CHIPS] for c in range(2)]
CORES = [[2 * z, 2 * z + 1] for z in range(16)]
NEIGHBOURS = [[8 * h + 2 * k + c for k in NEAR] for h in range(4) for c in range(2)]
GROUP = [[8 * h + i for i in OWNER] for h in range(4)]


def swap(values, axis, groups=None):
    return lax.all_to_all(values, axis, split_axis=0, concat_axis=0, axis_index_groups=groups)


def place(i, j):
    return (i * (i + 1) // 2 + j) * SIDE


def call(kernel, out_shape, flops, *operands, scratch=(), scalars=0):
    moved = sum(o.size * o.dtype.itemsize for o in operands)
    specs = [pl.BlockSpec(memory_space=pltpu.SMEM)] * scalars
    specs += [pl.BlockSpec(memory_space=pltpu.VMEM)] * (len(operands) - scalars)
    many = isinstance(out_shape, (list, tuple))
    whole = pl.BlockSpec(memory_space=pltpu.VMEM)
    return pl.pallas_call(
        kernel,
        out_shape=out_shape,
        in_specs=specs,
        out_specs=[whole] * len(out_shape) if many else whole,
        scratch_shapes=list(scratch),
        cost_estimate=pl.CostEstimate(flops=flops, bytes_accessed=moved, transcendentals=0),
        compiler_params=pltpu.CompilerParams(vmem_limit_bytes=16 * 1024 * 1024),
    )(*operands)


def spread_kernel(one_ref, two_ref, out_ref, held_ref, sems):
    refs = (one_ref, two_ref)
    copies = [pltpu.make_async_copy(refs[v], held_ref.at[v], sems.at[v]) for v in range(2)]
    for copy in copies:
        copy.start()
    for v in range(2):
        copies[v].wait()
        for k in range(SLICES):
            piece = held_ref[v, :, k * PART : (k + 1) * PART]
            for h in range(GROUPS):
                out_ref[CHIPS.index(h * SLICES + k), v] = piece


def normalize(values):
    values = values.astype(jnp.float32)
    center = jnp.sum(values, axis=0, keepdims=True) / BATCH
    shifted = values - center
    spread = jnp.sum(shifted * shifted, axis=0, keepdims=True) / BATCH
    scaling = lax.rsqrt(spread + EPSILON)
    return (shifted * scaling).astype(jnp.bfloat16), scaling


def gram_kernel(core_ref, whole_ref, mine_ref, other_ref, terms_ref, packed_ref):
    core = core_ref[0]
    other_ref[...], _ = normalize(whole_ref[:, :, 1 - core].reshape(BATCH, PART))
    row = lax.broadcasted_iota(jnp.int32, (SIDE, SIDE), 0)
    column = lax.broadcasted_iota(jnp.int32, (SIDE, SIDE), 1)
    mean_diag = jnp.where(row == column, float(PART), 0.0)
    for i in range(BLOCKS):
        left = other_ref[i * SIDE : (i + 1) * SIDE]
        for j in range(i + 1):
            right = other_ref[j * SIDE : (j + 1) * SIDE]
            block = lax.dot_general(left, right, NT, preferred_element_type=jnp.float32)
            if i == j:
                block = block - mean_diag
            packed_ref[place(i, j) : place(i, j) + SIDE] = block.astype(jnp.bfloat16)
    mine_ref[...], scaling = normalize(whole_ref[:, :, core].reshape(BATCH, PART))
    both = mine_ref[...].astype(jnp.float32) * other_ref[...].astype(jnp.float32)
    on_diag = jnp.sum(both, axis=0, keepdims=True) / BATCH
    terms_ref[0:1] = scaling
    terms_ref[1:2] = on_diag
    terms_ref[2:3] = -2.0 * (1.0 - on_diag) - 2.0 * LAMBDA * on_diag


def sum_kernel(parts_ref, out_ref):
    total = parts_ref[0].astype(jnp.float32)
    for k in range(1, parts_ref.shape[0]):
        total = total + parts_ref[k].astype(jnp.float32)
    total = total.astype(jnp.bfloat16)
    for k in range(out_ref.shape[0]):
        out_ref[k] = total


def apply_kernel(place_ref, packed_ref, mine_ref, other_ref, terms_ref, out_ref, up_ref):
    group = place_ref[0]
    mine = [mine_ref[i * SIDE : (i + 1) * SIDE] for i in range(BLOCKS)]
    scaling, on_diag, slope = terms_ref[0:1], terms_ref[1:2], terms_ref[2:3]
    zero = jnp.zeros((1, PART), jnp.float32)
    squares, first, second = zero, zero, zero
    for i in range(BLOCKS):
        held = mine[i].astype(jnp.float32)
        product = FEATURES * held
        for j in range(BLOCKS):
            if i >= j:
                block = packed_ref[place(i, j) : place(i, j) + SIDE]
                product = product + jnp.dot(block, mine[j], preferred_element_type=jnp.float32)
            else:
                block = packed_ref[place(j, i) : place(j, i) + SIDE]
                product = product + lax.dot_general(
                    block, mine[j], TN, preferred_element_type=jnp.float32
                )
        other = other_ref[i * SIDE : (i + 1) * SIDE].astype(jnp.float32)
        up = (2.0 * LAMBDA / BATCH) * product + slope * other
        up_ref[i * SIDE : (i + 1) * SIDE] = up
        squares = squares + jnp.sum(product * held, axis=0, keepdims=True)
        first = first + jnp.sum(up, axis=0, keepdims=True)
        second = second + jnp.sum(up * held, axis=0, keepdims=True)
    squares, first, second = squares / (BATCH * BATCH), first / BATCH, second / BATCH
    loss = (1.0 - on_diag) * (1.0 - on_diag) + LAMBDA * (squares - on_diag * on_diag)
    for k in range(SLICES):
        places = [CHIPS.index(h * SLICES + k) for h in range(GROUPS)]
        order = sum(jnp.where(group == h, places[h], 0) for h in range(GROUPS))
        for c in range(2):
            start = c * (BATCH // 2) + order * ROWS
            rows = pl.ds(pl.multiple_of(start, ROWS), ROWS)
            held = mine_ref[rows].astype(jnp.float32)
            grad = scaling * (up_ref[rows] - first - held * second)
            out_ref[OWNER.index(2 * k + c), :, :PART] = grad.astype(jnp.bfloat16)
    high = loss.astype(jnp.bfloat16)
    rest = loss - high.astype(jnp.float32)
    middle = rest.astype(jnp.bfloat16)
    low = (rest - middle.astype(jnp.float32)).astype(jnp.bfloat16)
    index = lax.broadcasted_iota(jnp.int32, (ROWS, SIDE), 0)
    tail = jnp.zeros((ROWS, SIDE), jnp.float32)
    for n, term in enumerate((high, middle, low)):
        for half in range(PART // SIDE):
            row = term[:, half * SIDE : (half + 1) * SIDE].astype(jnp.float32)
            tail = jnp.where(index == n * (PART // SIDE) + half, row, tail)
    tail = tail.astype(jnp.bfloat16)
    for k in range(2 * SLICES):
        out_ref[k, :, PART:] = tail


def unpack_kernel(parts_ref, loss_ref, one_ref, two_ref):
    halves = PART // SIDE
    for k in range(SLICES):
        columns = slice(k * PART, (k + 1) * PART)
        one_ref[:, columns] = parts_ref[OWNER.index(2 * k), :, :PART].astype(jnp.float32)
        two_ref[:, columns] = parts_ref[OWNER.index(2 * k + 1), :, :PART].astype(jnp.float32)
        tail = parts_ref[OWNER.index(2 * k), :, PART:].astype(jnp.float32)
        for half in range(halves):
            high, middle, low = [tail[n * halves + half : n * halves + half + 1] for n in range(3)]
            start = k * PART + half * SIDE
            loss_ref[:, start : start + SIDE] = high + (middle + low)


def local(view_one, view_two):
    bf16, f32 = jnp.bfloat16, jnp.float32
    shape = jax.ShapeDtypeStruct
    device = lax.axis_index("batch").astype(jnp.int32).reshape(1)
    core, group = device % 2, device // 8

    sent = pl.pallas_call(
        spread_kernel,
        out_shape=pltpu.VMEM((OWNERS, 2, ROWS, PART), bf16),
        in_specs=[pl.BlockSpec(memory_space=pl.ANY)] * 2,
        out_specs=pl.BlockSpec(memory_space=pltpu.VMEM),
        scratch_shapes=[pltpu.VMEM((2, ROWS, WIDTH), bf16), pltpu.SemaphoreType.DMA((2,))],
    )(view_one, view_two)
    sent, core, group = lax.optimization_barrier((sent, core, group))
    whole = lax.all_gather(swap(sent, "batch", SAME_CORE), "batch", axis_index_groups=CORES)

    mine, other, terms, packed = call(
        gram_kernel,
        [
            pltpu.VMEM((BATCH, PART), bf16),
            pltpu.VMEM((BATCH, PART), bf16),
            pltpu.VMEM((8, PART), f32),
            pltpu.VMEM((PACKED, SIDE), bf16),
        ],
        2 * BATCH * BATCH * PART,
        core,
        whole,
        scalars=1,
    )
    strips = swap(packed.reshape(OWNERS, CHUNK, SIDE), "feat", [list(FEAT)])
    strips = swap(call(sum_kernel, shape((SLICES, CHUNK, SIDE), bf16), 0, strips), "batch", NEIGHBOURS)
    strips = swap(call(sum_kernel, shape((OWNERS, CHUNK, SIDE), bf16), 0, strips), "feat", [list(FEAT)])

    out = call(
        apply_kernel,
        shape((2 * SLICES, ROWS, PART + SIDE), bf16),
        2 * BATCH * BATCH * PART,
        group,
        strips.reshape(PACKED, SIDE),
        mine,
        other,
        terms,
        scratch=[pltpu.VMEM((BATCH, PART), f32)],
        scalars=1,
    )
    loss, one, two = call(
        unpack_kernel,
        [shape((1, WIDTH), f32), shape((ROWS, WIDTH), f32), shape((ROWS, WIDTH), f32)],
        0,
        swap(out, "batch", GROUP),
    )
    return (loss.reshape(WIDTH), one, two)


def solution(mesh):
    spread = P("batch", "feat")
    return jax.shard_map(
        local, mesh=mesh, in_specs=(spread, spread), out_specs=(P("feat"), spread, spread), check_vma=False
    )
```

```python
import jax
import jax.numpy as jnp
from jax import lax
from jax.experimental import pallas as pl
from jax.experimental.pallas import tpu as pltpu
from jax.sharding import PartitionSpec as P

EPSILON = 1e-05
LAMBDA = 0.0051
FEATURES = 16384
BATCH = 512

CHIPS = (11, 12, 13, 14, 15, 0, 1, 2, 3, 4, 5, 6, 7, 8, 9, 10)
NEAR = (1, 2, 0, 3)
OWNER = (2, 3, 4, 5, 0, 1, 6, 7)
FEAT = (10, 11, 12, 13, 14, 15, 0, 1, 2, 3, 4, 5, 6, 7, 8, 9)
GROUPS = 4
SLICES = 4
OWNERS = 16
ROWS = 16
WIDTH = 1024
PART = WIDTH // SLICES
SIDE = 128
BLOCKS = BATCH // SIDE
PACKED = BLOCKS * (BLOCKS + 1) // 2 * SIDE
CHUNK = PACKED // OWNERS
NT = (((1,), (1,)), ((), ()))
TN = (((0,), (0,)), ((), ()))


SAME_CORE = [[2 * z + c for z in CHIPS] for c in range(2)]
CORES = [[2 * z, 2 * z + 1] for z in range(16)]
NEIGHBOURS = [[8 * h + 2 * k + c for k in NEAR] for h in range(4) for c in range(2)]
GROUP = [[8 * h + i for i in OWNER] for h in range(4)]


def swap(values, axis, groups=None):
    return lax.all_to_all(values, axis, split_axis=0, concat_axis=0, axis_index_groups=groups)


def place(i, j):
    return (i * (i + 1) // 2 + j) * SIDE


def call(kernel, out_shape, flops, *operands, scratch=(), scalars=0):
    moved = sum(o.size * o.dtype.itemsize for o in operands)
    specs = [pl.BlockSpec(memory_space=pltpu.SMEM)] * scalars
    specs += [pl.BlockSpec(memory_space=pltpu.VMEM)] * (len(operands) - scalars)
    many = isinstance(out_shape, (list, tuple))
    whole = pl.BlockSpec(memory_space=pltpu.VMEM)
    return pl.pallas_call(
        kernel,
        out_shape=out_shape,
        in_specs=specs,
        out_specs=[whole] * len(out_shape) if many else whole,
        scratch_shapes=list(scratch),
        cost_estimate=pl.CostEstimate(flops=flops, bytes_accessed=moved, transcendentals=0),
        compiler_params=pltpu.CompilerParams(vmem_limit_bytes=16 * 1024 * 1024),
    )(*operands)


def spread_kernel(one_ref, two_ref, out_ref, held_ref, sems):
    refs = (one_ref, two_ref)
    copies = [pltpu.make_async_copy(refs[v], held_ref.at[v], sems.at[v]) for v in range(2)]
    for copy in copies:
        copy.start()
    for v in range(2):
        copies[v].wait()
        for k in range(SLICES):
            piece = held_ref[v, :, k * PART : (k + 1) * PART]
            for h in range(GROUPS):
                out_ref[CHIPS.index(h * SLICES + k), v] = piece


def normalize(values):
    values = values.astype(jnp.float32)
    center = jnp.sum(values, axis=0, keepdims=True) / BATCH
    shifted = values - center
    spread = jnp.sum(shifted * shifted, axis=0, keepdims=True) / BATCH
    scaling = lax.rsqrt(spread + EPSILON)
    return (shifted * scaling).astype(jnp.bfloat16), scaling


def gram_kernel(core_ref, whole_ref, mine_ref, other_ref, terms_ref, packed_ref):
    core = core_ref[0]
    other_ref[...], _ = normalize(whole_ref[:, :, 1 - core].reshape(BATCH, PART))
    row = lax.broadcasted_iota(jnp.int32, (SIDE, SIDE), 0)
    column = lax.broadcasted_iota(jnp.int32, (SIDE, SIDE), 1)
    mean_diag = jnp.where(row == column, float(PART), 0.0)
    for i in range(BLOCKS):
        left = other_ref[i * SIDE : (i + 1) * SIDE]
        for j in range(i + 1):
            right = other_ref[j * SIDE : (j + 1) * SIDE]
            block = lax.dot_general(left, right, NT, preferred_element_type=jnp.float32)
            if i == j:
                block = block - mean_diag
            packed_ref[place(i, j) : place(i, j) + SIDE] = block.astype(jnp.bfloat16)
    mine_ref[...], scaling = normalize(whole_ref[:, :, core].reshape(BATCH, PART))
    both = mine_ref[...].astype(jnp.float32) * other_ref[...].astype(jnp.float32)
    on_diag = jnp.sum(both, axis=0, keepdims=True) / BATCH
    terms_ref[0:1] = scaling
    terms_ref[1:2] = on_diag
    terms_ref[2:3] = -2.0 * (1.0 - on_diag) - 2.0 * LAMBDA * on_diag


def sum_kernel(parts_ref, out_ref):
    total = parts_ref[0].astype(jnp.float32)
    for k in range(1, parts_ref.shape[0]):
        total = total + parts_ref[k].astype(jnp.float32)
    total = total.astype(jnp.bfloat16)
    for k in range(out_ref.shape[0]):
        out_ref[k] = total


def apply_kernel(place_ref, packed_ref, mine_ref, other_ref, terms_ref, out_ref, up_ref):
    group = place_ref[0]
    mine = [mine_ref[i * SIDE : (i + 1) * SIDE] for i in range(BLOCKS)]
    scaling, on_diag, slope = terms_ref[0:1], terms_ref[1:2], terms_ref[2:3]
    zero = jnp.zeros((1, PART), jnp.float32)
    squares, first, second = zero, zero, zero
    for i in range(BLOCKS):
        held = mine[i].astype(jnp.float32)
        product = FEATURES * held
        for j in range(BLOCKS):
            if i >= j:
                block = packed_ref[place(i, j) : place(i, j) + SIDE]
                product = product + jnp.dot(block, mine[j], preferred_element_type=jnp.float32)
            else:
                block = packed_ref[place(j, i) : place(j, i) + SIDE]
                product = product + lax.dot_general(
                    block, mine[j], TN, preferred_element_type=jnp.float32
                )
        other = other_ref[i * SIDE : (i + 1) * SIDE].astype(jnp.float32)
        up = (2.0 * LAMBDA / BATCH) * product + slope * other
        up_ref[i * SIDE : (i + 1) * SIDE] = up
        squares = squares + jnp.sum(product * held, axis=0, keepdims=True)
        first = first + jnp.sum(up, axis=0, keepdims=True)
        second = second + jnp.sum(up * held, axis=0, keepdims=True)
    squares, first, second = squares / (BATCH * BATCH), first / BATCH, second / BATCH
    loss = (1.0 - on_diag) * (1.0 - on_diag) + LAMBDA * (squares - on_diag * on_diag)
    for k in range(SLICES):
        places = [CHIPS.index(h * SLICES + k) for h in range(GROUPS)]
        order = sum(jnp.where(group == h, places[h], 0) for h in range(GROUPS))
        for c in range(2):
            start = c * (BATCH // 2) + order * ROWS
            rows = pl.ds(pl.multiple_of(start, ROWS), ROWS)
            held = mine_ref[rows].astype(jnp.float32)
            grad = scaling * (up_ref[rows] - first - held * second)
            out_ref[OWNER.index(2 * k + c), :, :PART] = grad.astype(jnp.bfloat16)
    high = loss.astype(jnp.bfloat16)
    rest = loss - high.astype(jnp.float32)
    middle = rest.astype(jnp.bfloat16)
    low = (rest - middle.astype(jnp.float32)).astype(jnp.bfloat16)
    index = lax.broadcasted_iota(jnp.int32, (ROWS, SIDE), 0)
    tail = jnp.zeros((ROWS, SIDE), jnp.float32)
    for n, term in enumerate((high, middle, low)):
        for half in range(PART // SIDE):
            row = term[:, half * SIDE : (half + 1) * SIDE].astype(jnp.float32)
            tail = jnp.where(index == n * (PART // SIDE) + half, row, tail)
    tail = tail.astype(jnp.bfloat16)
    for k in range(2 * SLICES):
        out_ref[k, :, PART:] = tail


def unpack_kernel(parts_ref, loss_ref, one_ref, two_ref):
    halves = PART // SIDE
    for k in range(SLICES):
        columns = slice(k * PART, (k + 1) * PART)
        one_ref[:, columns] = parts_ref[OWNER.index(2 * k), :, :PART].astype(jnp.float32)
        two_ref[:, columns] = parts_ref[OWNER.index(2 * k + 1), :, :PART].astype(jnp.float32)
        tail = parts_ref[OWNER.index(2 * k), :, PART:].astype(jnp.float32)
        for half in range(halves):
            high, middle, low = [tail[n * halves + half : n * halves + half + 1] for n in range(3)]
            start = k * PART + half * SIDE
            loss_ref[:, start : start + SIDE] = high + (middle + low)


def local(view_one, view_two):
    bf16, f32 = jnp.bfloat16, jnp.float32
    shape = jax.ShapeDtypeStruct
    device = lax.axis_index("batch").astype(jnp.int32).reshape(1)
    core, group = device % 2, device // 8

    sent = pl.pallas_call(
        spread_kernel,
        out_shape=pltpu.VMEM((OWNERS, 2, ROWS, PART), bf16),
        in_specs=[pl.BlockSpec(memory_space=pl.ANY)] * 2,
        out_specs=pl.BlockSpec(memory_space=pltpu.VMEM),
        scratch_shapes=[pltpu.VMEM((2, ROWS, WIDTH), bf16), pltpu.SemaphoreType.DMA((2,))],
    )(view_one, view_two)
    sent, core, group = lax.optimization_barrier((sent, core, group))
    whole = lax.all_gather(swap(sent, "batch", SAME_CORE), "batch", axis_index_groups=CORES)

    mine, other, terms, packed = call(
        gram_kernel,
        [
            pltpu.VMEM((BATCH, PART), bf16),
            pltpu.VMEM((BATCH, PART), bf16),
            pltpu.VMEM((8, PART), f32),
            pltpu.VMEM((PACKED, SIDE), bf16),
        ],
        2 * BATCH * BATCH * PART,
        core,
        whole,
        scalars=1,
    )
    strips = swap(packed.reshape(OWNERS, CHUNK, SIDE), "feat", [list(FEAT)])
    strips = swap(call(sum_kernel, shape((SLICES, CHUNK, SIDE), bf16), 0, strips), "batch", NEIGHBOURS)
    strips = swap(call(sum_kernel, shape((OWNERS, CHUNK, SIDE), bf16), 0, strips), "feat", [list(FEAT)])

    out = call(
        apply_kernel,
        shape((2 * SLICES, ROWS, PART + SIDE), bf16),
        2 * BATCH * BATCH * PART,
        group,
        strips.reshape(PACKED, SIDE),
        mine,
        other,
        terms,
        scratch=[pltpu.VMEM((BATCH, PART), f32)],
        scalars=1,
    )
    loss, one, two = call(
        unpack_kernel,
        [shape((1, WIDTH), f32), shape((ROWS, WIDTH), f32), shape((ROWS, WIDTH), f32)],
        0,
        swap(out, "batch", GROUP),
    )
    return (loss.reshape(WIDTH), one, two)


def solution(mesh):
    spread = P("batch", "feat")
    return jax.shard_map(
        local, mesh=mesh, in_specs=(spread, spread), out_specs=(P("feat"), spread, spread), check_vma=False
    )
```

```python
import jax
import jax.numpy as jnp
from jax import lax
from jax.experimental import pallas as pl
from jax.experimental.pallas import tpu as pltpu
from jax.sharding import PartitionSpec as P

EPSILON = 1e-05
LAMBDA = 0.0051
FEATURES = 16384
BATCH = 512

CHIPS = (12, 13, 14, 15, 0, 1, 2, 3, 4, 5, 6, 7, 8, 9, 10, 11)
NEAR = (1, 2, 0, 3)
OWNER = (2, 3, 4, 5, 0, 1, 6, 7)
FEAT = (10, 11, 12, 13, 14, 15, 0, 1, 2, 3, 4, 5, 6, 7, 8, 9)
GROUPS = 4
SLICES = 4
OWNERS = 16
ROWS = 16
WIDTH = 1024
PART = WIDTH // SLICES
SIDE = 128
BLOCKS = BATCH // SIDE
PACKED = BLOCKS * (BLOCKS + 1) // 2 * SIDE
CHUNK = PACKED // OWNERS
NT = (((1,), (1,)), ((), ()))
TN = (((0,), (0,)), ((), ()))


SAME_CORE = [[2 * z + c for z in CHIPS] for c in range(2)]
CORES = [[2 * z, 2 * z + 1] for z in range(16)]
NEIGHBOURS = [[8 * h + 2 * k + c for k in NEAR] for h in range(4) for c in range(2)]
GROUP = [[8 * h + i for i in OWNER] for h in range(4)]


def swap(values, axis, groups=None):
    return lax.all_to_all(values, axis, split_axis=0, concat_axis=0, axis_index_groups=groups)


def place(i, j):
    return (i * (i + 1) // 2 + j) * SIDE


def call(kernel, out_shape, flops, *operands, scratch=(), scalars=0):
    moved = sum(o.size * o.dtype.itemsize for o in operands)
    specs = [pl.BlockSpec(memory_space=pltpu.SMEM)] * scalars
    specs += [pl.BlockSpec(memory_space=pltpu.VMEM)] * (len(operands) - scalars)
    many = isinstance(out_shape, (list, tuple))
    whole = pl.BlockSpec(memory_space=pltpu.VMEM)
    return pl.pallas_call(
        kernel,
        out_shape=out_shape,
        in_specs=specs,
        out_specs=[whole] * len(out_shape) if many else whole,
        scratch_shapes=list(scratch),
        cost_estimate=pl.CostEstimate(flops=flops, bytes_accessed=moved, transcendentals=0),
        compiler_params=pltpu.CompilerParams(vmem_limit_bytes=16 * 1024 * 1024),
    )(*operands)


def spread_kernel(one_ref, two_ref, out_ref, held_ref, sems):
    refs = (one_ref, two_ref)
    copies = [pltpu.make_async_copy(refs[v], held_ref.at[v], sems.at[v]) for v in range(2)]
    for copy in copies:
        copy.start()
    for v in range(2):
        copies[v].wait()
        for k in range(SLICES):
            piece = held_ref[v, :, k * PART : (k + 1) * PART]
            for h in range(GROUPS):
                out_ref[CHIPS.index(h * SLICES + k), v] = piece


def normalize(values):
    values = values.astype(jnp.float32)
    center = jnp.sum(values, axis=0, keepdims=True) / BATCH
    shifted = values - center
    spread = jnp.sum(shifted * shifted, axis=0, keepdims=True) / BATCH
    scaling = lax.rsqrt(spread + EPSILON)
    return (shifted * scaling).astype(jnp.bfloat16), scaling


def gram_kernel(core_ref, whole_ref, mine_ref, other_ref, terms_ref, packed_ref):
    core = core_ref[0]
    other_ref[...], _ = normalize(whole_ref[:, :, 1 - core].reshape(BATCH, PART))
    row = lax.broadcasted_iota(jnp.int32, (SIDE, SIDE), 0)
    column = lax.broadcasted_iota(jnp.int32, (SIDE, SIDE), 1)
    mean_diag = jnp.where(row == column, float(PART), 0.0)
    for i in range(BLOCKS):
        left = other_ref[i * SIDE : (i + 1) * SIDE]
        for j in range(i + 1):
            right = other_ref[j * SIDE : (j + 1) * SIDE]
            block = lax.dot_general(left, right, NT, preferred_element_type=jnp.float32)
            if i == j:
                block = block - mean_diag
            packed_ref[place(i, j) : place(i, j) + SIDE] = block.astype(jnp.bfloat16)
    mine_ref[...], scaling = normalize(whole_ref[:, :, core].reshape(BATCH, PART))
    both = mine_ref[...].astype(jnp.float32) * other_ref[...].astype(jnp.float32)
    on_diag = jnp.sum(both, axis=0, keepdims=True) / BATCH
    terms_ref[0:1] = scaling
    terms_ref[1:2] = on_diag
    terms_ref[2:3] = -2.0 * (1.0 - on_diag) - 2.0 * LAMBDA * on_diag


def sum_kernel(parts_ref, out_ref):
    total = parts_ref[0].astype(jnp.float32)
    for k in range(1, parts_ref.shape[0]):
        total = total + parts_ref[k].astype(jnp.float32)
    total = total.astype(jnp.bfloat16)
    for k in range(out_ref.shape[0]):
        out_ref[k] = total


def apply_kernel(place_ref, packed_ref, mine_ref, other_ref, terms_ref, out_ref, up_ref):
    group = place_ref[0]
    mine = [mine_ref[i * SIDE : (i + 1) * SIDE] for i in range(BLOCKS)]
    scaling, on_diag, slope = terms_ref[0:1], terms_ref[1:2], terms_ref[2:3]
    zero = jnp.zeros((1, PART), jnp.float32)
    squares, first, second = zero, zero, zero
    for i in range(BLOCKS):
        held = mine[i].astype(jnp.float32)
        product = FEATURES * held
        for j in range(BLOCKS):
            if i >= j:
                block = packed_ref[place(i, j) : place(i, j) + SIDE]
                product = product + jnp.dot(block, mine[j], preferred_element_type=jnp.float32)
            else:
                block = packed_ref[place(j, i) : place(j, i) + SIDE]
                product = product + lax.dot_general(
                    block, mine[j], TN, preferred_element_type=jnp.float32
                )
        other = other_ref[i * SIDE : (i + 1) * SIDE].astype(jnp.float32)
        up = (2.0 * LAMBDA / BATCH) * product + slope * other
        up_ref[i * SIDE : (i + 1) * SIDE] = up
        squares = squares + jnp.sum(product * held, axis=0, keepdims=True)
        first = first + jnp.sum(up, axis=0, keepdims=True)
        second = second + jnp.sum(up * held, axis=0, keepdims=True)
    squares, first, second = squares / (BATCH * BATCH), first / BATCH, second / BATCH
    loss = (1.0 - on_diag) * (1.0 - on_diag) + LAMBDA * (squares - on_diag * on_diag)
    for k in range(SLICES):
        places = [CHIPS.index(h * SLICES + k) for h in range(GROUPS)]
        order = sum(jnp.where(group == h, places[h], 0) for h in range(GROUPS))
        for c in range(2):
            start = c * (BATCH // 2) + order * ROWS
            rows = pl.ds(pl.multiple_of(start, ROWS), ROWS)
            held = mine_ref[rows].astype(jnp.float32)
            grad = scaling * (up_ref[rows] - first - held * second)
            out_ref[OWNER.index(2 * k + c), :, :PART] = grad.astype(jnp.bfloat16)
    high = loss.astype(jnp.bfloat16)
    rest = loss - high.astype(jnp.float32)
    middle = rest.astype(jnp.bfloat16)
    low = (rest - middle.astype(jnp.float32)).astype(jnp.bfloat16)
    index = lax.broadcasted_iota(jnp.int32, (ROWS, SIDE), 0)
    tail = jnp.zeros((ROWS, SIDE), jnp.float32)
    for n, term in enumerate((high, middle, low)):
        for half in range(PART // SIDE):
            row = term[:, half * SIDE : (half + 1) * SIDE].astype(jnp.float32)
            tail = jnp.where(index == n * (PART // SIDE) + half, row, tail)
    tail = tail.astype(jnp.bfloat16)
    for k in range(2 * SLICES):
        out_ref[k, :, PART:] = tail


def unpack_kernel(parts_ref, loss_ref, one_ref, two_ref):
    halves = PART // SIDE
    for k in range(SLICES):
        columns = slice(k * PART, (k + 1) * PART)
        one_ref[:, columns] = parts_ref[OWNER.index(2 * k), :, :PART].astype(jnp.float32)
        two_ref[:, columns] = parts_ref[OWNER.index(2 * k + 1), :, :PART].astype(jnp.float32)
        tail = parts_ref[OWNER.index(2 * k), :, PART:].astype(jnp.float32)
        for half in range(halves):
            high, middle, low = [tail[n * halves + half : n * halves + half + 1] for n in range(3)]
            start = k * PART + half * SIDE
            loss_ref[:, start : start + SIDE] = high + (middle + low)


def local(view_one, view_two):
    bf16, f32 = jnp.bfloat16, jnp.float32
    shape = jax.ShapeDtypeStruct
    device = lax.axis_index("batch").astype(jnp.int32).reshape(1)
    core, group = device % 2, device // 8

    sent = pl.pallas_call(
        spread_kernel,
        out_shape=pltpu.VMEM((OWNERS, 2, ROWS, PART), bf16),
        in_specs=[pl.BlockSpec(memory_space=pl.ANY)] * 2,
        out_specs=pl.BlockSpec(memory_space=pltpu.VMEM),
        scratch_shapes=[pltpu.VMEM((2, ROWS, WIDTH), bf16), pltpu.SemaphoreType.DMA((2,))],
    )(view_one, view_two)
    sent, core, group = lax.optimization_barrier((sent, core, group))
    whole = lax.all_gather(swap(sent, "batch", SAME_CORE), "batch", axis_index_groups=CORES)

    mine, other, terms, packed = call(
        gram_kernel,
        [
            pltpu.VMEM((BATCH, PART), bf16),
            pltpu.VMEM((BATCH, PART), bf16),
            pltpu.VMEM((8, PART), f32),
            pltpu.VMEM((PACKED, SIDE), bf16),
        ],
        2 * BATCH * BATCH * PART,
        core,
        whole,
        scalars=1,
    )
    strips = swap(packed.reshape(OWNERS, CHUNK, SIDE), "feat", [list(FEAT)])
    strips = swap(call(sum_kernel, shape((SLICES, CHUNK, SIDE), bf16), 0, strips), "batch", NEIGHBOURS)
    strips = swap(call(sum_kernel, shape((OWNERS, CHUNK, SIDE), bf16), 0, strips), "feat", [list(FEAT)])

    out = call(
        apply_kernel,
        shape((2 * SLICES, ROWS, PART + SIDE), bf16),
        2 * BATCH * BATCH * PART,
        group,
        strips.reshape(PACKED, SIDE),
        mine,
        other,
        terms,
        scratch=[pltpu.VMEM((BATCH, PART), f32)],
        scalars=1,
    )
    loss, one, two = call(
        unpack_kernel,
        [shape((1, WIDTH), f32), shape((ROWS, WIDTH), f32), shape((ROWS, WIDTH), f32)],
        0,
        swap(out, "batch", GROUP),
    )
    return (loss.reshape(WIDTH), one, two)


def solution(mesh):
    spread = P("batch", "feat")
    return jax.shard_map(
        local, mesh=mesh, in_specs=(spread, spread), out_specs=(P("feat"), spread, spread), check_vma=False
    )
```

```python
import jax
import jax.numpy as jnp
from jax import lax
from jax.experimental import pallas as pl
from jax.experimental.pallas import tpu as pltpu
from jax.sharding import PartitionSpec as P

EPSILON = 1e-05
LAMBDA = 0.0051
FEATURES = 16384
BATCH = 512

CHIPS = (11, 12, 13, 14, 15, 0, 1, 2, 3, 4, 5, 6, 7, 8, 9, 10)
NEAR = (1, 2, 0, 3)
OWNER = (2, 3, 4, 5, 0, 1, 6, 7)
FEAT = (10, 11, 14, 15, 9, 8, 13, 12, 6, 7, 2, 3, 5, 4, 1, 0)
GROUPS = 4
SLICES = 4
OWNERS = 16
ROWS = 16
WIDTH = 1024
PART = WIDTH // SLICES
SIDE = 128
BLOCKS = BATCH // SIDE
PACKED = BLOCKS * (BLOCKS + 1) // 2 * SIDE
CHUNK = PACKED // OWNERS
NT = (((1,), (1,)), ((), ()))
TN = (((0,), (0,)), ((), ()))


SAME_CORE = [[2 * z + c for z in CHIPS] for c in range(2)]
CORES = [[2 * z, 2 * z + 1] for z in range(16)]
NEIGHBOURS = [[8 * h + 2 * k + c for k in NEAR] for h in range(4) for c in range(2)]
GROUP = [[8 * h + i for i in OWNER] for h in range(4)]


def swap(values, axis, groups=None):
    return lax.all_to_all(values, axis, split_axis=0, concat_axis=0, axis_index_groups=groups)


def place(i, j):
    return (i * (i + 1) // 2 + j) * SIDE


def call(kernel, out_shape, flops, *operands, scratch=(), scalars=0):
    moved = sum(o.size * o.dtype.itemsize for o in operands)
    specs = [pl.BlockSpec(memory_space=pltpu.SMEM)] * scalars
    specs += [pl.BlockSpec(memory_space=pltpu.VMEM)] * (len(operands) - scalars)
    many = isinstance(out_shape, (list, tuple))
    whole = pl.BlockSpec(memory_space=pltpu.VMEM)
    return pl.pallas_call(
        kernel,
        out_shape=out_shape,
        in_specs=specs,
        out_specs=[whole] * len(out_shape) if many else whole,
        scratch_shapes=list(scratch),
        cost_estimate=pl.CostEstimate(flops=flops, bytes_accessed=moved, transcendentals=0),
        compiler_params=pltpu.CompilerParams(vmem_limit_bytes=16 * 1024 * 1024),
    )(*operands)


def spread_kernel(one_ref, two_ref, out_ref, held_ref, sems):
    refs = (one_ref, two_ref)
    copies = [pltpu.make_async_copy(refs[v], held_ref.at[v], sems.at[v]) for v in range(2)]
    for copy in copies:
        copy.start()
    for v in range(2):
        copies[v].wait()
        for k in range(SLICES):
            piece = held_ref[v, :, k * PART : (k + 1) * PART]
            for h in range(GROUPS):
                out_ref[CHIPS.index(h * SLICES + k), v] = piece


def normalize(values):
    values = values.astype(jnp.float32)
    center = jnp.sum(values, axis=0, keepdims=True) / BATCH
    shifted = values - center
    spread = jnp.sum(shifted * shifted, axis=0, keepdims=True) / BATCH
    scaling = lax.rsqrt(spread + EPSILON)
    return (shifted * scaling).astype(jnp.bfloat16), scaling


def gram_kernel(core_ref, whole_ref, mine_ref, other_ref, terms_ref, packed_ref):
    core = core_ref[0]
    other_ref[...], _ = normalize(whole_ref[:, :, 1 - core].reshape(BATCH, PART))
    row = lax.broadcasted_iota(jnp.int32, (SIDE, SIDE), 0)
    column = lax.broadcasted_iota(jnp.int32, (SIDE, SIDE), 1)
    mean_diag = jnp.where(row == column, float(PART), 0.0)
    for i in range(BLOCKS):
        left = other_ref[i * SIDE : (i + 1) * SIDE]
        for j in range(i + 1):
            right = other_ref[j * SIDE : (j + 1) * SIDE]
            block = lax.dot_general(left, right, NT, preferred_element_type=jnp.float32)
            if i == j:
                block = block - mean_diag
            packed_ref[place(i, j) : place(i, j) + SIDE] = block.astype(jnp.bfloat16)
    mine_ref[...], scaling = normalize(whole_ref[:, :, core].reshape(BATCH, PART))
    both = mine_ref[...].astype(jnp.float32) * other_ref[...].astype(jnp.float32)
    on_diag = jnp.sum(both, axis=0, keepdims=True) / BATCH
    terms_ref[0:1] = scaling
    terms_ref[1:2] = on_diag
    terms_ref[2:3] = -2.0 * (1.0 - on_diag) - 2.0 * LAMBDA * on_diag


def sum_kernel(parts_ref, out_ref):
    total = parts_ref[0].astype(jnp.float32)
    for k in range(1, parts_ref.shape[0]):
        total = total + parts_ref[k].astype(jnp.float32)
    total = total.astype(jnp.bfloat16)
    for k in range(out_ref.shape[0]):
        out_ref[k] = total


def apply_kernel(place_ref, packed_ref, mine_ref, other_ref, terms_ref, out_ref, up_ref):
    group = place_ref[0]
    mine = [mine_ref[i * SIDE : (i + 1) * SIDE] for i in range(BLOCKS)]
    scaling, on_diag, slope = terms_ref[0:1], terms_ref[1:2], terms_ref[2:3]
    zero = jnp.zeros((1, PART), jnp.float32)
    squares, first, second = zero, zero, zero
    for i in range(BLOCKS):
        held = mine[i].astype(jnp.float32)
        product = FEATURES * held
        for j in range(BLOCKS):
            if i >= j:
                block = packed_ref[place(i, j) : place(i, j) + SIDE]
                product = product + jnp.dot(block, mine[j], preferred_element_type=jnp.float32)
            else:
                block = packed_ref[place(j, i) : place(j, i) + SIDE]
                product = product + lax.dot_general(
                    block, mine[j], TN, preferred_element_type=jnp.float32
                )
        other = other_ref[i * SIDE : (i + 1) * SIDE].astype(jnp.float32)
        up = (2.0 * LAMBDA / BATCH) * product + slope * other
        up_ref[i * SIDE : (i + 1) * SIDE] = up
        squares = squares + jnp.sum(product * held, axis=0, keepdims=True)
        first = first + jnp.sum(up, axis=0, keepdims=True)
        second = second + jnp.sum(up * held, axis=0, keepdims=True)
    squares, first, second = squares / (BATCH * BATCH), first / BATCH, second / BATCH
    loss = (1.0 - on_diag) * (1.0 - on_diag) + LAMBDA * (squares - on_diag * on_diag)
    for k in range(SLICES):
        places = [CHIPS.index(h * SLICES + k) for h in range(GROUPS)]
        order = sum(jnp.where(group == h, places[h], 0) for h in range(GROUPS))
        for c in range(2):
            start = c * (BATCH // 2) + order * ROWS
            rows = pl.ds(pl.multiple_of(start, ROWS), ROWS)
            held = mine_ref[rows].astype(jnp.float32)
            grad = scaling * (up_ref[rows] - first - held * second)
            out_ref[OWNER.index(2 * k + c), :, :PART] = grad.astype(jnp.bfloat16)
    high = loss.astype(jnp.bfloat16)
    rest = loss - high.astype(jnp.float32)
    middle = rest.astype(jnp.bfloat16)
    low = (rest - middle.astype(jnp.float32)).astype(jnp.bfloat16)
    index = lax.broadcasted_iota(jnp.int32, (ROWS, SIDE), 0)
    tail = jnp.zeros((ROWS, SIDE), jnp.float32)
    for n, term in enumerate((high, middle, low)):
        for half in range(PART // SIDE):
            row = term[:, half * SIDE : (half + 1) * SIDE].astype(jnp.float32)
            tail = jnp.where(index == n * (PART // SIDE) + half, row, tail)
    tail = tail.astype(jnp.bfloat16)
    for k in range(2 * SLICES):
        out_ref[k, :, PART:] = tail


def unpack_kernel(parts_ref, loss_ref, one_ref, two_ref):
    halves = PART // SIDE
    for k in range(SLICES):
        columns = slice(k * PART, (k + 1) * PART)
        one_ref[:, columns] = parts_ref[OWNER.index(2 * k), :, :PART].astype(jnp.float32)
        two_ref[:, columns] = parts_ref[OWNER.index(2 * k + 1), :, :PART].astype(jnp.float32)
        tail = parts_ref[OWNER.index(2 * k), :, PART:].astype(jnp.float32)
        for half in range(halves):
            high, middle, low = [tail[n * halves + half : n * halves + half + 1] for n in range(3)]
            start = k * PART + half * SIDE
            loss_ref[:, start : start + SIDE] = high + (middle + low)


def local(view_one, view_two):
    bf16, f32 = jnp.bfloat16, jnp.float32
    shape = jax.ShapeDtypeStruct
    device = lax.axis_index("batch").astype(jnp.int32).reshape(1)
    core, group = device % 2, device // 8

    sent = pl.pallas_call(
        spread_kernel,
        out_shape=pltpu.VMEM((OWNERS, 2, ROWS, PART), bf16),
        in_specs=[pl.BlockSpec(memory_space=pl.ANY)] * 2,
        out_specs=pl.BlockSpec(memory_space=pltpu.VMEM),
        scratch_shapes=[pltpu.VMEM((2, ROWS, WIDTH), bf16), pltpu.SemaphoreType.DMA((2,))],
    )(view_one, view_two)
    sent, core, group = lax.optimization_barrier((sent, core, group))
    whole = lax.all_gather(swap(sent, "batch", SAME_CORE), "batch", axis_index_groups=CORES)

    mine, other, terms, packed = call(
        gram_kernel,
        [
            pltpu.VMEM((BATCH, PART), bf16),
            pltpu.VMEM((BATCH, PART), bf16),
            pltpu.VMEM((8, PART), f32),
            pltpu.VMEM((PACKED, SIDE), bf16),
        ],
        2 * BATCH * BATCH * PART,
        core,
        whole,
        scalars=1,
    )
    strips = swap(packed.reshape(OWNERS, CHUNK, SIDE), "feat", [list(FEAT)])
    strips = swap(call(sum_kernel, shape((SLICES, CHUNK, SIDE), bf16), 0, strips), "batch", NEIGHBOURS)
    strips = swap(call(sum_kernel, shape((OWNERS, CHUNK, SIDE), bf16), 0, strips), "feat", [list(FEAT)])

    out = call(
        apply_kernel,
        shape((2 * SLICES, ROWS, PART + SIDE), bf16),
        2 * BATCH * BATCH * PART,
        group,
        strips.reshape(PACKED, SIDE),
        mine,
        other,
        terms,
        scratch=[pltpu.VMEM((BATCH, PART), f32)],
        scalars=1,
    )
    loss, one, two = call(
        unpack_kernel,
        [shape((1, WIDTH), f32), shape((ROWS, WIDTH), f32), shape((ROWS, WIDTH), f32)],
        0,
        swap(out, "batch", GROUP),
    )
    return (loss.reshape(WIDTH), one, two)


def solution(mesh):
    spread = P("batch", "feat")
    return jax.shard_map(
        local, mesh=mesh, in_specs=(spread, spread), out_specs=(P("feat"), spread, spread), check_vma=False
    )
```
